256 devices in a mesh: seq: 4 (over z_lo), res: 64 (over y, z_hi, x, core).
Axes of the slice: x: 4, y: 4, z: 8 (z_hi: 2, z_lo: 4; z = z_hi * 4 + z_lo), core: 2. Of those that a mesh axis runs over, the one named last changes fastest.
Arguments:
- sequence_features: bfloat16 [1024, 262144], P('seq', 'res'), may hold values from -6 to 6
- pair_window_rows: bfloat16 [256, 4096, 128], P('seq', 'res'), may hold values from -16 to 16
- residue_mask: int32 [4096], P('res'), may hold values 0 or 1
- sequence_validity: int32 [1024], P('seq'), may hold values 0 or 1
- pair_head_weight: bfloat16 [128, 8], replicated, may hold values from -16 to 16
- content_projection: bfloat16 [64, 64], replicated, may hold values from -0.75 to 0.75
- sigmoid_projection: bfloat16 [64, 64], replicated, may hold values from -0.75 to 0.75
- closing_projection: bfloat16 [64, 64], replicated, may hold values from -0.75 to 0.75
Outputs:
- updated: bfloat16 [1024, 16384], P('seq', 'res')
The draws below stay inside these ranges and needn't reach their ends.
All inputs are finite; a program needn't handle non-finite values. No bound on the sum of `residue_mask` or of `sequence_validity` on one device may be relied on, other than what follows from the above.
Results may differ from the reference program's by a relative error of at most 0.015.
The reference program's roundings to bfloat16 on the way count: a program that leaves them out, or rounds other values in their place, can miss the bound.
Values may be sent and summed in bfloat16 or wider, within the bound.
No kernel may reach another device: no remote copies, remote signals or barrier semaphores. Data moves between devices by JAX's collectives and lax.ppermute only.
A program may use at most 128 MiB of HBM per device.

```python
import jax
import jax.numpy as jnp
from jax import lax

FEATURE_DEPTH = 64
CZ = 128
HEADS = 8
HEAD_CHANNELS = 8
SHARD_POSITIONS = 64
SHARD_SPAN = 4
SEQUENCE_TOTAL = 1024
POSITION_TOTAL = 4096
SPAN_LENGTH = 256
N_RES = 64


def shared_direction(key):
    return jnp.clip(jax.random.normal(jax.random.fold_in(key, 77), (CZ, HEADS), jnp.float32), -4.0, 4.0)


def draw_pair_head_weight(key, part):
    directions = shared_direction(key)
    key = jax.random.fold_in(key, 1)
    factors = jax.random.uniform(key, (1, HEADS), jnp.float32, 0.6, 1.4)
    spread = 0.25
    return (directions * spread * factors).astype(jnp.bfloat16)


def draw_pair_window_rows(key, part):
    key = jax.random.fold_in(key, 2)
    key_base = jax.random.fold_in(key, 0)
    sample = jax.random.normal(key_base, (SPAN_LENGTH, POSITION_TOTAL, CZ), jnp.float32)
    return jnp.clip(sample, -16.0, 16.0).astype(jnp.bfloat16)


def plant(result, stream_key, low, largest):
    index_at = [jax.random.randint(jax.random.fold_in(stream_key, axis), (), 0, length) for axis, length in enumerate(result.shape)]
    main_axis = result.shape.index(max(result.shape))
    neighbour = index_at[:main_axis] + [(index_at[main_axis] + 1) % result.shape[main_axis]] + index_at[main_axis + 1:]
    return result.at[tuple(index_at)].set(low).at[tuple(neighbour)].set(largest)


def block_levels(own_key, shape, shards, smallest, largest):
    factor_of = 1.0
    for dim, blocks in shards:
        steps = jax.random.uniform(jax.random.fold_in(jax.random.fold_in(own_key, 6), dim), (blocks,), jnp.float32, smallest / len(shards), largest / len(shards))
        factor_of = factor_of * jnp.repeat(jnp.exp(steps), shape[dim] // blocks).reshape((-1,) + (1,) * (len(shape) - 1 - dim))
    return factor_of


def noise(own_key, shape, deviation, most, shards=(), held_as=jnp.bfloat16):
    gain = block_levels(own_key, shape, shards, -0.22, 0.18) if shards else 1.0
    drawn = jax.random.normal(own_key, shape, jnp.float32) * deviation * gain
    return jnp.minimum(jnp.maximum(drawn, -most), most).astype(held_as)


def setup_inputs(seed: int = 0) -> dict:
    streams_of = jax.random.split(jax.random.key(seed), 9)
    return {
        "sequence_features": noise(streams_of[0], (SEQUENCE_TOTAL, POSITION_TOTAL * FEATURE_DEPTH), 1.0, 6.0, ((0, 4), (1, 64))),
        "pair_window_rows": draw_pair_window_rows(jax.random.fold_in(streams_of[8], 71), 0),
        "residue_mask": plant((jax.random.randint(streams_of[2], (POSITION_TOTAL,), 0, 4) < 3).astype(jnp.int32), jax.random.fold_in(streams_of[2], 1), 0, 1),
        "sequence_validity": plant((jax.random.randint(streams_of[3], (SEQUENCE_TOTAL,), 0, 8) < 7).astype(jnp.int32), jax.random.fold_in(streams_of[3], 1), 0, 1),
        "pair_head_weight": draw_pair_head_weight(jax.random.fold_in(streams_of[8], 71), 0),
        "content_projection": noise(streams_of[5], (FEATURE_DEPTH, FEATURE_DEPTH), FEATURE_DEPTH ** -0.5, 0.75),
        "sigmoid_projection": noise(streams_of[6], (FEATURE_DEPTH, FEATURE_DEPTH), FEATURE_DEPTH ** -0.5, 0.75),
        "closing_projection": noise(streams_of[7], (FEATURE_DEPTH, FEATURE_DEPTH), FEATURE_DEPTH ** -0.5, 0.75),
    }


def layer_norm_apply(inputs):
    average = lax.optimization_barrier(jnp.mean(inputs, -1, keepdims=True))
    centered = inputs - average
    variance = lax.optimization_barrier(jnp.mean(centered * centered, -1, keepdims=True))
    return centered * lax.rsqrt(variance + 1e-05)

def pair_weights(tile_block, residue_mask, pair_head_weight):
    block_rows = tile_block.shape[0]
    normed_pair = layer_norm_apply(tile_block.astype(jnp.float32)).astype(jnp.bfloat16)
    logits = jnp.dot(normed_pair.reshape(-1, CZ), pair_head_weight, preferred_element_type=jnp.float32)
    logits = logits.reshape(block_rows, POSITION_TOTAL, HEADS)
    logits = jnp.where(residue_mask[None, :, None] == 1, logits, -1000000000.0)
    row_top = lax.optimization_barrier(jnp.max(logits, axis=1, keepdims=True))
    exponents = jnp.exp(logits - row_top)
    totals = lax.optimization_barrier(jnp.sum(exponents, axis=1, keepdims=True))
    return (exponents / totals).astype(jnp.bfloat16)

def reference(sequence_features, pair_window_rows, residue_mask, sequence_validity, pair_head_weight, content_projection, sigmoid_projection, closing_projection):
    tile_blocks = pair_window_rows.reshape(SPAN_LENGTH // 16, 16, POSITION_TOTAL, CZ)
    weights = lax.map(lambda tile_block: pair_weights(tile_block, residue_mask, pair_head_weight), tile_blocks)
    weights = weights.reshape(SPAN_LENGTH, POSITION_TOTAL, HEADS)
    sequence_extent = sequence_features.reshape(SEQUENCE_TOTAL, POSITION_TOTAL, FEATURE_DEPTH)
    standardized_features = layer_norm_apply(sequence_extent.astype(jnp.float32)).astype(jnp.bfloat16)
    mapped_update = jnp.dot(standardized_features.reshape(-1, FEATURE_DEPTH), content_projection, preferred_element_type=jnp.float32)
    mapped_update = mapped_update.reshape(SEQUENCE_TOTAL, POSITION_TOTAL, FEATURE_DEPTH) * sequence_validity[:, None, None].astype(jnp.float32)
    values = mapped_update.astype(jnp.bfloat16)

    def head_mix(head_index):
        value_per_head = lax.dynamic_slice_in_dim(values, head_index * HEAD_CHANNELS, HEAD_CHANNELS, 2)
        head_weights = lax.dynamic_slice_in_dim(weights, head_index, 1, 2)[:, :, 0]
        right_operand = value_per_head.transpose(1, 0, 2).reshape(POSITION_TOTAL, SEQUENCE_TOTAL * HEAD_CHANNELS)
        summed_heads = jnp.dot(head_weights, right_operand, preferred_element_type=jnp.float32)
        return summed_heads.reshape(SPAN_LENGTH, SEQUENCE_TOTAL, HEAD_CHANNELS)
    coupling_mean = lax.map(head_mix, jnp.arange(HEADS, dtype=jnp.int32))
    coupling_mean = coupling_mean.transpose(2, 1, 0, 3).reshape(SEQUENCE_TOTAL, SPAN_LENGTH, FEATURE_DEPTH)
    span_sequences = standardized_features.reshape(SEQUENCE_TOTAL, N_RES, SHARD_POSITIONS, FEATURE_DEPTH)[:, :, :SHARD_SPAN].reshape(SEQUENCE_TOTAL, SPAN_LENGTH, FEATURE_DEPTH)
    sigmoid_factor = jax.nn.sigmoid(jnp.dot(span_sequences.reshape(-1, FEATURE_DEPTH), sigmoid_projection, preferred_element_type=jnp.float32))
    filtered_update = (sigmoid_factor.reshape(SEQUENCE_TOTAL, SPAN_LENGTH, FEATURE_DEPTH) * coupling_mean).astype(jnp.bfloat16)
    returned_update = jnp.dot(filtered_update.reshape(-1, FEATURE_DEPTH), closing_projection, preferred_element_type=jnp.float32)
    return returned_update.astype(jnp.bfloat16).reshape(SEQUENCE_TOTAL, SPAN_LENGTH * FEATURE_DEPTH)
```

```python
import functools

import jax
import jax.numpy as jnp
from jax import lax
from jax.experimental import pallas as pl
from jax.experimental.pallas import tpu as pltpu
from jax.sharding import Mesh
from jax.sharding import PartitionSpec as P

F32 = jnp.float32
BF16 = jnp.bfloat16
EPS = 1e-05
NT = (((1,), (1,)), ((), ()))
NN = (((1,), (0,)), ((), ()))
TN = (((0,), (0,)), ((), ()))
GROUP = ("y", "x")
RES = ("y", "zh", "x", "core")
VMEM_LIMIT = 48 * 1024 * 1024


def dot(a, b, dims=NN):
    return lax.dot_general(a, b, dims, preferred_element_type=F32)


def iota(shape, dim):
    return lax.broadcasted_iota(jnp.int32, shape, dim)


def one_hot(cond):
    return jnp.where(cond, 1.0, 0.0).astype(BF16)


def logits_kernel(pair_ref, mask_ref, weight_ref, out_ref, scr):
    rows = pair_ref.shape[0] * pair_ref.shape[1]
    step = pl.program_id(0)
    x = pair_ref[...].reshape(rows, 128)
    mean_m = jnp.full((128, 128), 1.0 / 128, BF16)
    centered = x.astype(F32) - dot(x, mean_m)
    square = centered * centered
    high = square.astype(BF16)
    low = (square - high.astype(F32)).astype(BF16)
    variance = dot(high, mean_m) + dot(low, mean_m)
    normed = (centered * lax.rsqrt(variance + EPS)).astype(BF16)
    logits = lax.dot_general(
        weight_ref[...], normed, NT, preferred_element_type=F32
    )
    mask = mask_ref[...]
    for k in range(rows // 128):
        part = jnp.where(mask == 1, logits[:, k * 128 : (k + 1) * 128], -1000000000.0)
        scr[pl.ds(k, 8, stride=rows // 128), :] = part
    block = scr[...].reshape(8, rows // 128, 128)
    for sg in range(2):
        out_ref[:, sg, pl.ds(step * (rows // 128), rows // 128), :] = block


def pair_logits(pair, mask2, weight_t):
    steps = 4
    return pl.pallas_call(
        logits_kernel,
        grid=(steps,),
        out_shape=jax.ShapeDtypeStruct((8, 2, 32, 128), F32),
        in_specs=[
            pl.BlockSpec((64 // steps, 64, 128), lambda i: (i, 0, 0)),
            pl.BlockSpec((1, 128), lambda i: (0, 0)),
            pl.BlockSpec((8, 128), lambda i: (0, 0)),
        ],
        out_specs=pl.BlockSpec((8, 2, 32, 128), lambda i: (0, 0, 0, 0)),
        scratch_shapes=[pltpu.VMEM((64 * 32 // 8 // steps, 128), F32)],
        compiler_params=pltpu.CompilerParams(vmem_limit_bytes=VMEM_LIMIT),
        cost_estimate=pl.CostEstimate(
            flops=400_000_000, bytes_accessed=1_400_000, transcendentals=500_000
        ),
        name="pair_logits",
    )(pair, mask2, weight_t)


def values_kernel(m_ref, valid_ref, content_ref, sigmoid_ref, v_ref, gate_ref, wbig):
    step = pl.program_id(0)

    @pl.when(step == 0)
    def _():
        spread = one_hot(iota((512, 64), 0) // 8 == iota((512, 64), 1))
        rep = dot(spread, content_ref[...], NT).astype(BF16)
        tile = one_hot(iota((64, 512), 1) % 64 == iota((64, 512), 0))
        full = dot(rep, tile)
        keep = iota((512, 512), 0) % 8 == iota((512, 512), 1) // 64
        wbig[...] = jnp.where(keep, full, 0.0).astype(BF16)

    eye = one_hot(iota((256, 256), 0) == iota((256, 256), 1))
    parts = []
    for k in range(4):
        xt = dot(eye, m_ref[:, k * 256 : (k + 1) * 256], NT).reshape(4, 64, 256)
        mean = jnp.sum(xt, axis=1, keepdims=True) * (1.0 / 64)
        centered = xt - mean
        variance = jnp.sum(centered * centered, axis=1, keepdims=True) * (1.0 / 64)
        parts.append((centered * lax.rsqrt(variance + EPS)).astype(BF16).reshape(256, 256))
    valid = valid_ref[...].astype(F32)
    halves = []
    for k in range(2):
        normed = jnp.concatenate(parts[2 * k : 2 * k + 2], axis=0)
        halves.append((dot(wbig[...], normed) * valid).reshape(64, 8, 256))
    both = jnp.concatenate(halves, axis=1).astype(BF16).reshape(8, 8, 16, 256)
    v_ref[:, 0] = both[..., :128]
    v_ref[:, 1] = both[..., 128:]

    @pl.when(step == 0)
    def _():
        spread = one_hot(iota((256, 64), 0) % 64 == iota((256, 64), 1))
        rep = dot(spread, sigmoid_ref[...], NT).astype(BF16)
        tile = one_hot(iota((64, 256), 1) % 64 == iota((64, 256), 0))
        full = dot(rep, tile)
        keep = iota((256, 256), 0) // 64 == iota((256, 256), 1) // 64
        wgate = jnp.where(keep, full, 0.0).astype(BF16)
        gate_ref[...] = jax.nn.sigmoid(dot(wgate, parts[0]))


def msa_values(m, valid, content, sigmoid):
    return pl.pallas_call(
        values_kernel,
        grid=(4,),
        out_shape=(
            jax.ShapeDtypeStruct((8, 2, 8, 64, 128), BF16),
            jax.ShapeDtypeStruct((256, 256), F32),
        ),
        in_specs=[
            pl.BlockSpec((256, 1024), lambda i: (0, i)),
            pl.BlockSpec((1, 256), lambda i: (0, 0)),
            pl.BlockSpec((64, 64), lambda i: (0, 0)),
            pl.BlockSpec((64, 64), lambda i: (0, 0)),
        ],
        out_specs=(
            pl.BlockSpec((8, 2, 8, 16, 128), lambda i: (0, 0, 0, i, 0)),
            pl.BlockSpec((256, 256), lambda i: (0, 0)),
        ),
        scratch_shapes=[pltpu.VMEM((512, 512), BF16)],
        compiler_params=pltpu.CompilerParams(vmem_limit_bytes=VMEM_LIMIT),
        cost_estimate=pl.CostEstimate(
            flops=2_000_000_000, bytes_accessed=4_500_000, transcendentals=100_000
        ),
        name="msa_values",
    )(m, valid, content, sigmoid)


def by_halves(x, reduce):
    low = iota(x.shape, 1) < 64
    a = reduce(x[:, :64], axis=1, keepdims=True)
    b = reduce(x[:, 64:], axis=1, keepdims=True)
    return jnp.where(low, a, b)


def stats_kernel(l_ref, out_ref):
    logits = l_ref[...]
    top = by_halves(jnp.max(logits, axis=0), jnp.max)
    total = by_halves(jnp.sum(jnp.exp(logits - top[None]), axis=0), jnp.sum)
    out_ref[0] = top
    out_ref[1] = total


def local_stats(logits):
    return pl.pallas_call(
        stats_kernel,
        out_shape=jax.ShapeDtypeStruct((2, 32, 128), F32),
        cost_estimate=pl.CostEstimate(
            flops=200_000, bytes_accessed=300_000, transcendentals=65536
        ),
        name="local_stats",
    )(logits)


def weights_kernel(l_ref, a_ref, b_ref, c_ref, d_ref, out_ref):
    refs = (a_ref, b_ref, c_ref, d_ref)
    top = jnp.maximum(
        jnp.maximum(a_ref[0], b_ref[0]), jnp.maximum(c_ref[0], d_ref[0])
    )
    total = sum(r[1] * jnp.exp(r[0] - top) for r in refs)
    low = iota((32, 128), 1) < 64
    for k in range(8):
        a = jnp.exp(l_ref[2 * k] - top) / total
        b = jnp.exp(l_ref[2 * k + 1] - top) / total
        even = jnp.where(low, a, pltpu.roll(b, 64, 1))
        odd = jnp.where(low, pltpu.roll(a, 64, 1), b)
        out_ref[0:32, k * 128 : (k + 1) * 128] = even.astype(BF16)
        out_ref[32:64, k * 128 : (k + 1) * 128] = odd.astype(BF16)


def softmax_weights(logits, stats):
    return pl.pallas_call(
        weights_kernel,
        out_shape=jax.ShapeDtypeStruct((64, 1024), BF16),
        cost_estimate=pl.CostEstimate(
            flops=200_000, bytes_accessed=500_000, transcendentals=65536
        ),
        name="softmax_weights",
    )(logits, *stats)


def average_kernel(place_ref, w0, w1, w2, w3, v_ref, out_ref, wall, scr):
    for k, w in enumerate((w0, w1, w2, w3)):
        start = pl.multiple_of(place_ref[k] * 64, 64)
        wall[pl.ds(start, 64), :] = w[...]
    weights = wall[...]
    for c2 in range(4):
        right = jnp.concatenate(
            [v_ref[:, 2 * c2 + e].reshape(1024, 128) for e in range(2)], axis=1
        )
        part = dot(weights, right)
        for e in range(2):
            for q in range(4):
                for par in range(2):
                    row = q * 64 + par * 32
                    scr[pl.ds((q * 64 + par) * 8 + 2 * c2 + e, 32, stride=16), :] = part[
                        row : row + 32, e * 128 : (e + 1) * 128
                    ]
    out_ref[...] = scr[...].astype(BF16).reshape(64, 32, 128)


def partial_average(place, weights, values):
    vmem = pl.BlockSpec(memory_space=pltpu.VMEM)
    return pl.pallas_call(
        average_kernel,
        out_shape=jax.ShapeDtypeStruct((64, 32, 128), BF16),
        in_specs=[pl.BlockSpec(memory_space=pltpu.SMEM)] + [vmem] * 5,
        out_specs=vmem,
        scratch_shapes=[pltpu.VMEM((256, 1024), BF16), pltpu.VMEM((2048, 128), F32)],
        compiler_params=pltpu.CompilerParams(vmem_limit_bytes=VMEM_LIMIT),
        cost_estimate=pl.CostEstimate(
            flops=600_000_000, bytes_accessed=3_100_000, transcendentals=0
        ),
        name="partial_average",
    )(place, *weights, values)


def closing_kernel(p_ref, gate_ref, closing_ref, out_ref, gated):
    for y in range(4):
        for x in range(4):
            head, half = 2 * y + x // 2, x % 2
            total = sum(
                p_ref[y * 16 + zh * 8 + x * 2 + core].astype(F32)
                for zh in range(2)
                for core in range(2)
            )
            cols = slice(half * 128, half * 128 + 128)
            for i in range(4):
                rows = slice(i * 64 + head * 8, i * 64 + head * 8 + 8)
                gated[rows, cols] = total[i * 8 : i * 8 + 8] * gate_ref[rows, cols]
    spread = one_hot(iota((256, 64), 0) % 64 == iota((256, 64), 1))
    rep = dot(spread, closing_ref[...]).astype(BF16)
    tile = one_hot(iota((64, 256), 1) % 64 == iota((64, 256), 0))
    full = dot(rep, tile)
    keep = iota((256, 256), 0) // 64 == iota((256, 256), 1) // 64
    block = jnp.where(keep, full, 0.0).astype(BF16)
    out_ref[...] = dot(gated[...].astype(BF16), block, TN).astype(BF16)


def close(parts, gate, closing):
    return pl.pallas_call(
        closing_kernel,
        out_shape=jax.ShapeDtypeStruct((256, 256), BF16),
        scratch_shapes=[pltpu.VMEM((256, 256), F32)],
        cost_estimate=pl.CostEstimate(
            flops=60_000_000, bytes_accessed=1_000_000, transcendentals=0
        ),
        name="closing",
    )(parts, gate, closing)


def exchange(x, axes):
    return lax.all_to_all(x, axes, split_axis=0, concat_axis=0, tiled=True)


def shards(
    sequence_features,
    pair_window_rows,
    residue_mask,
    sequence_validity,
    pair_head_weight,
    content_projection,
    sigmoid_projection,
    closing_projection,
):
    mask2 = jnp.concatenate([residue_mask, residue_mask]).reshape(1, 128)
    logits = pair_logits(pair_window_rows, mask2, pair_head_weight.T)
    logits = exchange(logits.reshape(16, 32, 128), GROUP)
    values, gate = msa_values(
        sequence_features,
        sequence_validity.reshape(1, 256),
        content_projection,
        sigmoid_projection,
    )
    values = exchange(values.reshape(16, 512, 128), GROUP)
    mine = local_stats(logits)
    swap = ((0, 1), (1, 0))
    both = tuple((k, 3 - k) for k in range(4))
    stats = (
        mine,
        lax.ppermute(mine, "core", swap),
        lax.ppermute(mine, "zh", swap),
        lax.ppermute(mine, ("zh", "core"), both),
    )
    weights = softmax_weights(logits, stats)
    gathered = [weights] + [
        lax.ppermute(weights, "seq", [(k, (k + d) % 4) for k in range(4)])
        for d in (1, 2, 3)
    ]
    q = lax.axis_index("seq")
    place = (q - jnp.arange(4, dtype=jnp.int32)) % 4
    parts = partial_average(place, gathered, values.reshape(16, 8, 64, 128))
    parts = exchange(parts, RES)
    return close(parts, gate, closing_projection)


def solution(mesh):
    fine = Mesh(mesh.devices.reshape(4, 4, 2, 4, 2), ("seq",) + RES)
    return jax.shard_map(
        shards,
        mesh=fine,
        in_specs=(
            P("seq", RES),
            P("seq", RES, None),
            P(RES),
            P("seq"),
            P(),
            P(),
            P(),
            P(),
        ),
        out_specs=P("seq", RES),
        check_vma=False,
    )
```

```python
import functools

import jax
import jax.numpy as jnp
from jax import lax
from jax.experimental import pallas as pl
from jax.experimental.pallas import tpu as pltpu
from jax.sharding import Mesh
from jax.sharding import PartitionSpec as P

F32 = jnp.float32
BF16 = jnp.bfloat16
EPS = 1e-05
NT = (((1,), (1,)), ((), ()))
NN = (((1,), (0,)), ((), ()))
TN = (((0,), (0,)), ((), ()))
GROUP = ("y", "x")
RES = ("y", "zh", "x", "core")
SMALL_LIMIT = 24 * 1024 * 1024


def dot(a, b, dims=NN):
    return lax.dot_general(a, b, dims, preferred_element_type=F32)


def iota(shape, dim):
    return lax.broadcasted_iota(jnp.int32, shape, dim)


def one_hot(cond):
    return jnp.where(cond, 1.0, 0.0).astype(BF16)


def logits_kernel(pair_ref, mask_ref, weight_ref, out_ref, scr):
    rows = pair_ref.shape[0] * pair_ref.shape[1]
    step = pl.program_id(0)
    x = pair_ref[...].reshape(rows, 128)
    mean_m = jnp.full((128, 128), 1.0 / 128, BF16)
    centered = x.astype(F32) - dot(x, mean_m)
    square = centered * centered
    high = square.astype(BF16)
    low = (square - high.astype(F32)).astype(BF16)
    variance = dot(high, mean_m) + dot(low, mean_m)
    normed = (centered * lax.rsqrt(variance + EPS)).astype(BF16)
    logits = lax.dot_general(
        weight_ref[...], normed, NT, preferred_element_type=F32
    )
    mask = jnp.concatenate([mask_ref[...], mask_ref[...]], axis=1)
    for k in range(rows // 128):
        part = jnp.where(mask == 1, logits[:, k * 128 : (k + 1) * 128], -1000000000.0)
        scr[pl.ds(k, 8, stride=rows // 128), :] = part
    block = scr[...].reshape(8, rows // 128, 128)
    for sg in range(2):
        out_ref[:, sg, pl.ds(step * (rows // 128), rows // 128), :] = block


def pair_logits(pair, mask, weight_t):
    steps = 4
    return pl.pallas_call(
        logits_kernel,
        grid=(steps,),
        out_shape=jax.ShapeDtypeStruct((8, 2, 32, 128), F32),
        in_specs=[
            pl.BlockSpec((64 // steps, 64, 128), lambda i: (i, 0, 0)),
            pl.BlockSpec((1, 64), lambda i: (0, 0)),
            pl.BlockSpec((8, 128), lambda i: (0, 0)),
        ],
        out_specs=pl.BlockSpec((8, 2, 32, 128), lambda i: (0, 0, 0, 0)),
        scratch_shapes=[pltpu.VMEM((64 * 32 // 8 // steps, 128), F32)],
        cost_estimate=pl.CostEstimate(
            flops=400_000_000, bytes_accessed=1_400_000, transcendentals=500_000
        ),
        name="pair_logits",
    )(pair, mask, weight_t)


def values_kernel(m_ref, valid_ref, content_ref, sigmoid_ref, v_ref, gate_ref, wbig):
    step = pl.program_id(0)

    @pl.when(step == 0)
    def _():
        spread = one_hot(iota((512, 64), 0) // 8 == iota((512, 64), 1))
        rep = dot(spread, content_ref[...], NT).astype(BF16)
        tile = one_hot(iota((64, 512), 1) % 64 == iota((64, 512), 0))
        full = dot(rep, tile)
        keep = iota((512, 512), 0) % 8 == iota((512, 512), 1) // 64
        wbig[...] = jnp.where(keep, full, 0.0).astype(BF16)

    eye = one_hot(iota((256, 256), 0) == iota((256, 256), 1))
    parts = []
    for k in range(4):
        xt = dot(eye, m_ref[:, k * 256 : (k + 1) * 256], NT).reshape(4, 64, 256)
        mean = jnp.sum(xt, axis=1, keepdims=True) * (1.0 / 64)
        centered = xt - mean
        variance = jnp.sum(centered * centered, axis=1, keepdims=True) * (1.0 / 64)
        parts.append((centered * lax.rsqrt(variance + EPS)).astype(BF16).reshape(256, 256))
    valid = valid_ref[...].astype(F32)
    halves = []
    for k in range(2):
        normed = jnp.concatenate(parts[2 * k : 2 * k + 2], axis=0)
        halves.append((dot(wbig[...], normed) * valid).reshape(64, 8, 256))
    both = jnp.concatenate(halves, axis=1).astype(BF16).reshape(8, 8, 16, 256)
    v_ref[:, 0] = both[..., :128]
    v_ref[:, 1] = both[..., 128:]

    @pl.when(step == 0)
    def _():
        spread = one_hot(iota((256, 64), 0) % 64 == iota((256, 64), 1))
        rep = dot(spread, sigmoid_ref[...], NT).astype(BF16)
        tile = one_hot(iota((64, 256), 1) % 64 == iota((64, 256), 0))
        full = dot(rep, tile)
        keep = iota((256, 256), 0) // 64 == iota((256, 256), 1) // 64
        wgate = jnp.where(keep, full, 0.0).astype(BF16)
        gate_ref[...] = jax.nn.sigmoid(dot(wgate, parts[0]))


def msa_values(m, valid, content, sigmoid):
    return pl.pallas_call(
        values_kernel,
        grid=(4,),
        out_shape=(
            jax.ShapeDtypeStruct((8, 2, 8, 64, 128), BF16),
            jax.ShapeDtypeStruct((256, 256), F32),
        ),
        in_specs=[
            pl.BlockSpec((256, 1024), lambda i: (0, i)),
            pl.BlockSpec((1, 256), lambda i: (0, 0)),
            pl.BlockSpec((64, 64), lambda i: (0, 0)),
            pl.BlockSpec((64, 64), lambda i: (0, 0)),
        ],
        out_specs=(
            pl.BlockSpec((8, 2, 8, 16, 128), lambda i: (0, 0, 0, i, 0)),
            pl.BlockSpec((256, 256), lambda i: (0, 0)),
        ),
        scratch_shapes=[pltpu.VMEM((512, 512), BF16)],
        cost_estimate=pl.CostEstimate(
            flops=2_000_000_000, bytes_accessed=4_500_000, transcendentals=100_000
        ),
        name="msa_values",
    )(m, valid, content, sigmoid)


def by_halves(x, reduce):
    low = iota(x.shape, 1) < 64
    a = reduce(x[:, :64], axis=1, keepdims=True)
    b = reduce(x[:, 64:], axis=1, keepdims=True)
    return jnp.where(low, a, b)


def stats_kernel(l_ref, out_ref):
    logits = l_ref[...]
    top = by_halves(jnp.max(logits, axis=0), jnp.max)
    total = by_halves(jnp.sum(jnp.exp(logits - top[None]), axis=0), jnp.sum)
    out_ref[0] = top
    out_ref[1] = total


def local_stats(logits):
    return pl.pallas_call(
        stats_kernel,
        out_shape=jax.ShapeDtypeStruct((2, 32, 128), F32),
        compiler_params=pltpu.CompilerParams(vmem_limit_bytes=SMALL_LIMIT),
        cost_estimate=pl.CostEstimate(
            flops=200_000, bytes_accessed=300_000, transcendentals=65536
        ),
        name="local_stats",
    )(logits)


def weights_kernel(l_ref, a_ref, b_ref, c_ref, d_ref, out_ref, own_ref):
    refs = (a_ref, b_ref, c_ref, d_ref)
    top = jnp.maximum(
        jnp.maximum(a_ref[0], b_ref[0]), jnp.maximum(c_ref[0], d_ref[0])
    )
    total = sum(r[1] * jnp.exp(r[0] - top) for r in refs)
    low = iota((32, 128), 1) < 64
    for k in range(8):
        a = jnp.exp(l_ref[2 * k] - top) / total
        b = jnp.exp(l_ref[2 * k + 1] - top) / total
        even = jnp.where(low, a, pltpu.roll(b, 64, 1))
        odd = jnp.where(low, pltpu.roll(a, 64, 1), b)
        block = jnp.concatenate([even, odd], axis=0).astype(BF16)
        out_ref[:, k * 128 : (k + 1) * 128] = block
        own_ref[:, k * 128 : (k + 1) * 128] = block


def softmax_weights(logits, stats):
    return pl.pallas_call(
        weights_kernel,
        out_shape=(jax.ShapeDtypeStruct((64, 1024), BF16),) * 2,
        compiler_params=pltpu.CompilerParams(vmem_limit_bytes=SMALL_LIMIT),
        cost_estimate=pl.CostEstimate(
            flops=200_000, bytes_accessed=500_000, transcendentals=65536
        ),
        name="softmax_weights",
    )(logits, *stats)


def average_kernel(place_ref, w0, w1, w2, w3, v_ref, out_ref, wall, scr):
    for k, w in enumerate((w0, w1, w2, w3)):
        start = pl.multiple_of(place_ref[k] * 64, 64)
        wall[pl.ds(start, 64), :] = w[...]
    weights = wall[...]
    for c2 in range(4):
        right = jnp.concatenate(
            [v_ref[:, 2 * c2 + e].reshape(1024, 128) for e in range(2)], axis=1
        )
        part = dot(weights, right)
        for e in range(2):
            for q in range(4):
                for par in range(2):
                    row = q * 64 + par * 32
                    scr[pl.ds((q * 64 + par) * 8 + 2 * c2 + e, 32, stride=16), :] = part[
                        row : row + 32, e * 128 : (e + 1) * 128
                    ]
    out_ref[...] = scr[...].astype(BF16).reshape(64, 32, 128)


def partial_average(place, weights, values):
    vmem = pl.BlockSpec(memory_space=pltpu.VMEM)
    return pl.pallas_call(
        average_kernel,
        out_shape=jax.ShapeDtypeStruct((64, 32, 128), BF16),
        in_specs=[pl.BlockSpec(memory_space=pltpu.SMEM)] + [vmem] * 5,
        out_specs=vmem,
        scratch_shapes=[pltpu.VMEM((256, 1024), BF16), pltpu.VMEM((2048, 128), F32)],
        compiler_params=pltpu.CompilerParams(vmem_limit_bytes=SMALL_LIMIT),
        cost_estimate=pl.CostEstimate(
            flops=600_000_000, bytes_accessed=3_100_000, transcendentals=0
        ),
        name="partial_average",
    )(place, *weights, values)


def closing_kernel(p_ref, gate_ref, closing_ref, out_ref, gated):
    for y in range(4):
        for x in range(4):
            head, half = 2 * y + x // 2, x % 2
            total = sum(
                p_ref[y * 16 + zh * 8 + x * 2 + core].astype(F32)
                for zh in range(2)
                for core in range(2)
            )
            cols = slice(half * 128, half * 128 + 128)
            for i in range(4):
                rows = slice(i * 64 + head * 8, i * 64 + head * 8 + 8)
                gated[rows, cols] = total[i * 8 : i * 8 + 8] * gate_ref[rows, cols]
    spread = one_hot(iota((256, 64), 0) % 64 == iota((256, 64), 1))
    rep = dot(spread, closing_ref[...]).astype(BF16)
    tile = one_hot(iota((64, 256), 1) % 64 == iota((64, 256), 0))
    full = dot(rep, tile)
    keep = iota((256, 256), 0) // 64 == iota((256, 256), 1) // 64
    block = jnp.where(keep, full, 0.0).astype(BF16)
    out_ref[...] = dot(gated[...].astype(BF16), block, TN).astype(BF16)


def close(parts, gate, closing):
    return pl.pallas_call(
        closing_kernel,
        out_shape=jax.ShapeDtypeStruct((256, 256), BF16),
        scratch_shapes=[pltpu.VMEM((256, 256), F32)],
        compiler_params=pltpu.CompilerParams(vmem_limit_bytes=SMALL_LIMIT),
        cost_estimate=pl.CostEstimate(
            flops=60_000_000, bytes_accessed=1_000_000, transcendentals=0
        ),
        name="closing",
    )(parts, gate, closing)


def exchange(x, axes):
    return lax.all_to_all(x, axes, split_axis=0, concat_axis=0, tiled=True)


def shards(
    sequence_features,
    pair_window_rows,
    residue_mask,
    sequence_validity,
    pair_head_weight,
    content_projection,
    sigmoid_projection,
    closing_projection,
):
    logits = pair_logits(pair_window_rows, residue_mask.reshape(1, 64), pair_head_weight.T)
    logits = exchange(logits.reshape(16, 32, 128), GROUP)
    values, gate = msa_values(
        sequence_features,
        sequence_validity.reshape(1, 256),
        content_projection,
        sigmoid_projection,
    )
    values = exchange(values.reshape(16, 512, 128), GROUP)
    mine = local_stats(logits)
    swap = ((0, 1), (1, 0))
    both = tuple((k, 3 - k) for k in range(4))
    stats = (
        mine,
        lax.ppermute(mine, "core", swap),
        lax.ppermute(mine, "zh", swap),
        lax.ppermute(mine, ("zh", "core"), both),
    )
    weights, own = softmax_weights(logits, stats)
    gathered = [own] + [
        lax.ppermute(weights, "seq", [(k, (k + d) % 4) for k in range(4)])
        for d in (1, 2, 3)
    ]
    q = lax.axis_index("seq")
    place = (q - jnp.arange(4, dtype=jnp.int32)) % 4
    parts = partial_average(place, gathered, values.reshape(16, 8, 64, 128))
    parts = exchange(parts, RES)
    return close(parts, gate, closing_projection)


def solution(mesh):
    fine = Mesh(mesh.devices.reshape(4, 4, 2, 4, 2), ("seq",) + RES)
    return jax.shard_map(
        shards,
        mesh=fine,
        in_specs=(
            P("seq", RES),
            P("seq", RES, None),
            P(RES),
            P("seq"),
            P(),
            P(),
            P(),
            P(),
        ),
        out_specs=P("seq", RES),
        check_vma=False,
    )
```

```python
import functools

import jax
import jax.numpy as jnp
from jax import lax
from jax.experimental import pallas as pl
from jax.experimental.pallas import tpu as pltpu
from jax.sharding import Mesh
from jax.sharding import PartitionSpec as P

F32 = jnp.float32
BF16 = jnp.bfloat16
EPS = 1e-05
NT = (((1,), (1,)), ((), ()))
NN = (((1,), (0,)), ((), ()))
TN = (((0,), (0,)), ((), ()))
GROUP = ("y", "x")
CHIPS = ("y", "zh", "x")
RES = CHIPS + ("core",)
SMALL_LIMIT = 24 * 1024 * 1024


def dot(a, b, dims=NN):
    return lax.dot_general(a, b, dims, preferred_element_type=F32)


def iota(shape, dim):
    return lax.broadcasted_iota(jnp.int32, shape, dim)


def one_hot(cond):
    return jnp.where(cond, 1.0, 0.0).astype(BF16)


def logits_kernel(pair_ref, mask_ref, weight_ref, out_ref, scr):
    rows = pair_ref.shape[0] * pair_ref.shape[1]
    step = pl.program_id(0)
    x = pair_ref[...].reshape(rows, 128)
    mean_m = jnp.full((128, 128), 1.0 / 128, BF16)
    centered = x.astype(F32) - dot(x, mean_m)
    square = centered * centered
    high = square.astype(BF16)
    low = (square - high.astype(F32)).astype(BF16)
    variance = dot(high, mean_m) + dot(low, mean_m)
    normed = (centered * lax.rsqrt(variance + EPS)).astype(BF16)
    logits = dot(weight_ref[...], normed, NT)
    mask = jnp.concatenate([mask_ref[...], mask_ref[...]], axis=1)
    for k in range(rows // 128):
        part = jnp.where(mask == 1, logits[:, k * 128 : (k + 1) * 128], -1000000000.0)
        row = step * (rows // 256) + (k // 2 % 2) * 16 + k // 4 * 2 + k % 2
        scr[pl.ds(row, 8, stride=32), :] = part

    @pl.when(step == pl.num_programs(0) - 1)
    def _():
        block = scr[...].reshape(8, 32, 128)
        for sg in range(2):
            out_ref[:, sg] = block


def pair_logits(pair, mask, weight_t):
    steps = 4
    return pl.pallas_call(
        logits_kernel,
        grid=(steps,),
        out_shape=jax.ShapeDtypeStruct((8, 2, 32, 128), F32),
        in_specs=[
            pl.BlockSpec((64 // steps, 64, 128), lambda i: (i, 0, 0)),
            pl.BlockSpec((1, 64), lambda i: (0, 0)),
            pl.BlockSpec((8, 128), lambda i: (0, 0)),
        ],
        out_specs=pl.BlockSpec((8, 2, 32, 128), lambda i: (0, 0, 0, 0)),
        scratch_shapes=[pltpu.VMEM((256, 128), F32)],
        cost_estimate=pl.CostEstimate(
            flops=400_000_000, bytes_accessed=1_400_000, transcendentals=500_000
        ),
        name="pair_logits",
    )(pair, mask, weight_t)


def values_kernel(m_ref, valid_ref, content_ref, sigmoid_ref, v_ref, gate_ref, wbig):
    step = pl.program_id(0)

    @pl.when(step == 0)
    def _():
        spread = one_hot(iota((512, 64), 0) // 8 == iota((512, 64), 1))
        rep = dot(spread, content_ref[...], NT).astype(BF16)
        tile = one_hot(iota((64, 512), 1) % 64 == iota((64, 512), 0))
        full = dot(rep, tile)
        keep = iota((512, 512), 0) % 8 == iota((512, 512), 1) // 64
        wbig[...] = jnp.where(keep, full, 0.0).astype(BF16)

    eye = one_hot(iota((256, 256), 0) == iota((256, 256), 1))
    parts = []
    for k in range(4):
        xt = dot(eye, m_ref[:, k * 256 : (k + 1) * 256], NT).reshape(4, 64, 256)
        mean = jnp.sum(xt, axis=1, keepdims=True) * (1.0 / 64)
        centered = xt - mean
        variance = jnp.sum(centered * centered, axis=1, keepdims=True) * (1.0 / 64)
        parts.append((centered * lax.rsqrt(variance + EPS)).astype(BF16).reshape(256, 256))
    halves = []
    for k in range(2):
        normed = jnp.concatenate(parts[2 * k : 2 * k + 2], axis=0)
        halves.append(dot(wbig[...], normed).reshape(64, 8, 256))
    both = jnp.concatenate(halves, axis=1).astype(BF16).reshape(8, 8, 16, 256)
    v_ref[:, 0] = both[..., :128]
    v_ref[:, 1] = both[..., 128:]

    @pl.when(step == 0)
    def _():
        spread = one_hot(iota((256, 64), 0) % 64 == iota((256, 64), 1))
        rep = dot(spread, sigmoid_ref[...], NT).astype(BF16)
        tile = one_hot(iota((64, 256), 1) % 64 == iota((64, 256), 0))
        full = dot(rep, tile)
        keep = iota((256, 256), 0) // 64 == iota((256, 256), 1) // 64
        wgate = jnp.where(keep, full, 0.0).astype(BF16)
        gate_ref[...] = jax.nn.sigmoid(dot(wgate, parts[0])) * valid_ref[...].astype(F32)


def msa_values(m, valid, content, sigmoid):
    return pl.pallas_call(
        values_kernel,
        grid=(4,),
        out_shape=(
            jax.ShapeDtypeStruct((8, 2, 8, 64, 128), BF16),
            jax.ShapeDtypeStruct((256, 256), F32),
        ),
        in_specs=[
            pl.BlockSpec((256, 1024), lambda i: (0, i)),
            pl.BlockSpec((1, 256), lambda i: (0, 0)),
            pl.BlockSpec((64, 64), lambda i: (0, 0)),
            pl.BlockSpec((64, 64), lambda i: (0, 0)),
        ],
        out_specs=(
            pl.BlockSpec((8, 2, 8, 16, 128), lambda i: (0, 0, 0, i, 0)),
            pl.BlockSpec((256, 256), lambda i: (0, 0)),
        ),
        scratch_shapes=[pltpu.VMEM((512, 512), BF16)],
        cost_estimate=pl.CostEstimate(
            flops=2_000_000_000, bytes_accessed=4_500_000, transcendentals=100_000
        ),
        name="msa_values",
    )(m, valid, content, sigmoid)


def by_halves(x, reduce):
    low = iota(x.shape, 1) < 64
    a = reduce(x[:, :64], axis=1, keepdims=True)
    b = reduce(x[:, 64:], axis=1, keepdims=True)
    return jnp.where(low, a, b)


def stats_kernel(l_ref, out_ref):
    logits = l_ref[...]
    top = by_halves(jnp.max(logits, axis=0), jnp.max)
    total = by_halves(jnp.sum(jnp.exp(logits - top[None]), axis=0), jnp.sum)
    out_ref[0] = top
    out_ref[1] = total


def local_stats(logits):
    return pl.pallas_call(
        stats_kernel,
        out_shape=jax.ShapeDtypeStruct((2, 32, 128), F32),
        compiler_params=pltpu.CompilerParams(vmem_limit_bytes=SMALL_LIMIT),
        cost_estimate=pl.CostEstimate(
            flops=200_000, bytes_accessed=300_000, transcendentals=65536
        ),
        name="local_stats",
    )(logits)


def merge(a, b):
    top = jnp.maximum(a[0], b[0])
    return top, a[1] * jnp.exp(a[0] - top) + b[1] * jnp.exp(b[0] - top)


def merge_kernel(a_ref, b_ref, out_ref):
    out_ref[0], out_ref[1] = merge(a_ref, b_ref)


def merge_stats(a, b):
    return pl.pallas_call(
        merge_kernel,
        out_shape=jax.ShapeDtypeStruct((2, 32, 128), F32),
        compiler_params=pltpu.CompilerParams(vmem_limit_bytes=SMALL_LIMIT),
        cost_estimate=pl.CostEstimate(
            flops=20_000, bytes_accessed=100_000, transcendentals=8192
        ),
        name="merge_stats",
    )(a, b)


def weights_kernel(l_ref, a_ref, b_ref, out_ref, own_ref):
    top, total = merge(a_ref, b_ref)
    low = iota((32, 128), 1) < 64
    for k in range(8):
        a = jnp.exp(l_ref[2 * k] - top) / total
        b = jnp.exp(l_ref[2 * k + 1] - top) / total
        even = jnp.where(low, a, pltpu.roll(b, 64, 1))
        odd = jnp.where(low, pltpu.roll(a, 64, 1), b)
        block = jnp.concatenate([even[:16], odd[:16], even[16:], odd[16:]], axis=0)
        block = block.astype(BF16)
        out_ref[:, k * 128 : (k + 1) * 128] = block
        own_ref[:, k * 128 : (k + 1) * 128] = block


def softmax_weights(logits, a, b):
    return pl.pallas_call(
        weights_kernel,
        out_shape=(jax.ShapeDtypeStruct((64, 1024), BF16),) * 2,
        compiler_params=pltpu.CompilerParams(vmem_limit_bytes=SMALL_LIMIT),
        cost_estimate=pl.CostEstimate(
            flops=200_000, bytes_accessed=500_000, transcendentals=65536
        ),
        name="softmax_weights",
    )(logits, a, b)


def average_kernel(place_ref, w0, w1, w2, w3, v_ref, out_ref, wall, scr):
    side = pl.multiple_of(place_ref[4] * 32, 32)
    for k, w in enumerate((w0, w1, w2, w3)):
        start = pl.multiple_of(place_ref[k] * 32, 32)
        wall[pl.ds(start, 32), :] = w[pl.ds(side, 32), :]
    weights = wall[...]
    for c2 in range(4):
        right = jnp.concatenate(
            [v_ref[:, 2 * c2 + e].reshape(1024, 128) for e in range(2)], axis=1
        )
        part = dot(weights, right)
        for e in range(2):
            for q in range(4):
                for par in range(2):
                    row = q * 32 + par * 16
                    scr[pl.ds(q * 256 + par * 8 + 2 * c2 + e, 16, stride=16), :] = part[
                        row : row + 16, e * 128 : (e + 1) * 128
                    ]
    out_ref[...] = scr[...].astype(out_ref.dtype).reshape(32, 32, 128)


def partial_average(place, weights, values, dtype):
    vmem = pl.BlockSpec(memory_space=pltpu.VMEM)
    return pl.pallas_call(
        average_kernel,
        out_shape=jax.ShapeDtypeStruct((32, 32, 128), dtype),
        in_specs=[pl.BlockSpec(memory_space=pltpu.SMEM)] + [vmem] * 5,
        out_specs=vmem,
        scratch_shapes=[pltpu.VMEM((128, 1024), BF16), pltpu.VMEM((1024, 128), F32)],
        compiler_params=pltpu.CompilerParams(vmem_limit_bytes=SMALL_LIMIT),
        cost_estimate=pl.CostEstimate(
            flops=300_000_000, bytes_accessed=2_800_000, transcendentals=0
        ),
        name="partial_average",
    )(place, *weights, values)


def add_kernel(a_ref, b_ref, out_ref):
    out_ref[...] = (a_ref[...] + b_ref[...].astype(F32)).astype(BF16)


def add_cores(a, b):
    return pl.pallas_call(
        add_kernel,
        out_shape=jax.ShapeDtypeStruct((32, 32, 128), BF16),
        compiler_params=pltpu.CompilerParams(vmem_limit_bytes=SMALL_LIMIT),
        cost_estimate=pl.CostEstimate(
            flops=200_000, bytes_accessed=1_000_000, transcendentals=0
        ),
        name="add_cores",
    )(a, b)


def closing_kernel(p_ref, gate_ref, closing_ref, out_ref, gated):
    for y in range(4):
        for x in range(4):
            head, half = 2 * y + x // 2, x % 2
            total = p_ref[y * 8 + x].astype(F32) + p_ref[y * 8 + 4 + x].astype(F32)
            cols = slice(half * 128, half * 128 + 128)
            for i in range(4):
                rows = slice(i * 64 + head * 8, i * 64 + head * 8 + 8)
                gated[rows, cols] = total[i * 8 : i * 8 + 8] * gate_ref[rows, cols]
    spread = one_hot(iota((256, 64), 0) % 64 == iota((256, 64), 1))
    rep = dot(spread, closing_ref[...]).astype(BF16)
    tile = one_hot(iota((64, 256), 1) % 64 == iota((64, 256), 0))
    full = dot(rep, tile)
    keep = iota((256, 256), 0) // 64 == iota((256, 256), 1) // 64
    block = jnp.where(keep, full, 0.0).astype(BF16)
    out_ref[...] = dot(gated[...].astype(BF16), block, TN).astype(BF16)


def close(parts, gate, closing):
    return pl.pallas_call(
        closing_kernel,
        out_shape=jax.ShapeDtypeStruct((256, 256), BF16),
        scratch_shapes=[pltpu.VMEM((256, 256), F32)],
        compiler_params=pltpu.CompilerParams(vmem_limit_bytes=SMALL_LIMIT),
        cost_estimate=pl.CostEstimate(
            flops=60_000_000, bytes_accessed=1_000_000, transcendentals=0
        ),
        name="closing",
    )(parts, gate, closing)


def exchange(x, axes):
    return lax.all_to_all(x, axes, split_axis=0, concat_axis=0, tiled=True)


def shards(
    sequence_features,
    pair_window_rows,
    residue_mask,
    sequence_validity,
    pair_head_weight,
    content_projection,
    sigmoid_projection,
    closing_projection,
):
    logits = pair_logits(pair_window_rows, residue_mask.reshape(1, 64), pair_head_weight.T)
    logits = exchange(logits.reshape(16, 32, 128), GROUP)
    values, gate = msa_values(
        sequence_features,
        sequence_validity.reshape(1, 256),
        content_projection,
        sigmoid_projection,
    )
    values = exchange(values.reshape(16, 512, 128), GROUP)
    swap = ((0, 1), (1, 0))
    mine = local_stats(logits)
    mine = merge_stats(mine, lax.ppermute(mine, "core", swap))
    weights, own = softmax_weights(logits, mine, lax.ppermute(mine, "zh", swap))
    gathered = [own] + [
        lax.ppermute(weights, "seq", [(k, (k + d) % 4) for k in range(4)])
        for d in (1, 2, 3)
    ]
    q, core = lax.axis_index("seq"), lax.axis_index("core")
    order = [(q - d) % 4 for d in range(4)]
    values = values.reshape(16, 8, 64, 128)
    theirs = partial_average(jnp.stack(order + [1 - core]), gathered, values, BF16)
    theirs = lax.ppermute(theirs, "core", swap)
    ours = partial_average(jnp.stack(order + [core]), gathered, values, F32)
    parts = exchange(add_cores(ours, theirs), CHIPS)
    return close(parts, gate, closing_projection)


def solution(mesh):
    fine = Mesh(mesh.devices.reshape(4, 4, 2, 4, 2), ("seq",) + RES)
    return jax.shard_map(
        shards,
        mesh=fine,
        in_specs=(
            P("seq", RES),
            P("seq", RES, None),
            P(RES),
            P("seq"),
            P(),
            P(),
            P(),
            P(),
        ),
        out_specs=P("seq", RES),
        check_vma=False,
    )
```

```python
import functools

import jax
import jax.numpy as jnp
from jax import lax
from jax.experimental import pallas as pl
from jax.experimental.pallas import tpu as pltpu
from jax.sharding import Mesh
from jax.sharding import PartitionSpec as P

F32 = jnp.float32
BF16 = jnp.bfloat16
EPS = 1e-05
NT = (((1,), (1,)), ((), ()))
NN = (((1,), (0,)), ((), ()))
TN = (((0,), (0,)), ((), ()))
GROUP = ("y", "x")
CHIPS = ("y", "zh", "x")
RES = CHIPS + ("core",)
SMALL_LIMIT = 24 * 1024 * 1024


def dot(a, b, dims=NN):
    return lax.dot_general(a, b, dims, preferred_element_type=F32)


def iota(shape, dim):
    return lax.broadcasted_iota(jnp.int32, shape, dim)


def one_hot(cond):
    return jnp.where(cond, 1.0, 0.0).astype(BF16)


def logits_kernel(pair_ref, mask_ref, weight_ref, out_ref, scr):
    x = pair_ref[...].reshape(4096, 128)
    centered = x.astype(F32) - dot(x, jnp.full((128, 128), 1.0 / 128, BF16))
    variance = jnp.mean(centered * centered, axis=-1, keepdims=True)
    normed = (centered * lax.rsqrt(variance + EPS)).astype(BF16)
    logits = dot(weight_ref[...], normed, NT)
    mask = jnp.concatenate([mask_ref[...], mask_ref[...]], axis=1)
    for k in range(32):
        part = jnp.where(mask == 1, logits[:, k * 128 : (k + 1) * 128], -1000000000.0)
        row = (k // 2 % 2) * 16 + k // 4 * 2 + k % 2
        scr[pl.ds(row, 8, stride=32), :] = part
    block = scr[...].reshape(8, 32, 128)
    for sg in range(2):
        out_ref[:, sg] = block


def pair_logits(pair, mask, weight_t):
    return pl.pallas_call(
        logits_kernel,
        grid=(1,),
        out_shape=jax.ShapeDtypeStruct((8, 2, 32, 128), F32),
        in_specs=[
            pl.BlockSpec((64, 64, 128), lambda i: (0, 0, 0)),
            pl.BlockSpec((1, 64), lambda i: (0, 0)),
            pl.BlockSpec((8, 128), lambda i: (0, 0)),
        ],
        out_specs=pl.BlockSpec((8, 2, 32, 128), lambda i: (0, 0, 0, 0)),
        scratch_shapes=[pltpu.VMEM((256, 128), F32)],
        cost_estimate=pl.CostEstimate(
            flops=400_000_000, bytes_accessed=1_400_000, transcendentals=500_000
        ),
        name="pair_logits",
    )(pair, mask, weight_t)


def diagonal(matrix, transposed=False, by_column=False):
    rows = iota((256, 64), 0)
    spread = one_hot((rows // 4 if by_column else rows % 64) == iota((256, 64), 1))
    rep = dot(spread, matrix, NT if transposed else NN).astype(BF16)
    tile = one_hot(iota((64, 256), 1) % 64 == iota((64, 256), 0))
    copy = iota((256, 256), 0)
    copy = copy % 4 if by_column else copy // 64
    return jnp.where(copy == iota((256, 256), 1) // 64, dot(rep, tile), 0.0).astype(BF16)


def normed_columns(block):
    xt = block.T.astype(F32).reshape(4, 64, 256)
    mean = jnp.sum(xt, axis=1, keepdims=True) * (1.0 / 64)
    centered = xt - mean
    variance = jnp.sum(centered * centered, axis=1, keepdims=True) * (1.0 / 64)
    return (centered * lax.rsqrt(variance + EPS)).astype(BF16).reshape(256, 256)


def values_kernel(m_ref, content_ref, v_ref, block):
    @pl.when(pl.program_id(0) == 0)
    def _():
        block[...] = diagonal(content_ref[...], transposed=True, by_column=True)

    low = iota((32, 8, 256), 1) < 4
    for part in range(m_ref.shape[1] // 1024):
        eights = []
        for k in range(2):
            start = part * 1024 + k * 512
            a, b = (
                dot(block[...], normed_columns(m_ref[:, at : at + 256])).reshape(32, 8, 256)
                for at in (start, start + 256)
            )
            even = jnp.where(low, a, pltpu.roll(b, 4, 1))
            odd = jnp.where(low, pltpu.roll(a, 4, 1), b)
            eights.append(jnp.stack([even, odd], axis=1).reshape(64, 8, 256))
        both = jnp.concatenate(eights, axis=1).astype(BF16).reshape(8, 8, 16, 256)
        rows = slice(part * 16, part * 16 + 16)
        v_ref[:, 0, :, rows] = both[..., :128]
        v_ref[:, 1, :, rows] = both[..., 128:]


def msa_values(m, content):
    return pl.pallas_call(
        values_kernel,
        grid=(2,),
        out_shape=jax.ShapeDtypeStruct((8, 2, 8, 64, 128), BF16),
        in_specs=[
            pl.BlockSpec((256, 2048), lambda i: (0, i)),
            pl.BlockSpec((64, 64), lambda i: (0, 0)),
        ],
        out_specs=pl.BlockSpec((8, 2, 8, 32, 128), lambda i: (0, 0, 0, i, 0)),
        scratch_shapes=[pltpu.VMEM((256, 256), BF16)],
        cost_estimate=pl.CostEstimate(
            flops=2_000_000_000, bytes_accessed=4_500_000, transcendentals=100_000
        ),
        name="msa_values",
    )(m, content)


def gate_kernel(m_ref, valid_ref, sigmoid_ref, closing_ref, gate_ref, block_ref):
    inner = dot(diagonal(sigmoid_ref[...], transposed=True), normed_columns(m_ref[...]))
    gate_ref[...] = jax.nn.sigmoid(inner) * valid_ref[...].astype(F32)
    block_ref[...] = diagonal(closing_ref[...])


def msa_gate(m, valid, sigmoid, closing):
    whole = lambda i: (0, 0)
    return pl.pallas_call(
        gate_kernel,
        grid=(1,),
        out_shape=(
            jax.ShapeDtypeStruct((256, 256), F32),
            jax.ShapeDtypeStruct((256, 256), BF16),
        ),
        in_specs=[
            pl.BlockSpec((256, 256), whole),
            pl.BlockSpec((1, 256), whole),
            pl.BlockSpec((64, 64), whole),
            pl.BlockSpec((64, 64), whole),
        ],
        out_specs=(pl.BlockSpec((256, 256), whole), pl.BlockSpec((256, 256), whole)),
        cost_estimate=pl.CostEstimate(
            flops=100_000_000, bytes_accessed=600_000, transcendentals=100_000
        ),
        name="msa_gate",
    )(m, valid, sigmoid, closing)


def by_halves(x, reduce):
    low = iota(x.shape, 1) < 64
    a = reduce(x[:, :64], axis=1, keepdims=True)
    b = reduce(x[:, 64:], axis=1, keepdims=True)
    return jnp.where(low, a, b)


def stats_kernel(l_ref, out_ref):
    logits = l_ref[...]
    top = by_halves(jnp.max(logits, axis=0), jnp.max)
    total = by_halves(jnp.sum(jnp.exp(logits - top[None]), axis=0), jnp.sum)
    out_ref[0] = top
    out_ref[1] = total


def local_stats(logits):
    return pl.pallas_call(
        stats_kernel,
        out_shape=jax.ShapeDtypeStruct((2, 32, 128), F32),
        compiler_params=pltpu.CompilerParams(vmem_limit_bytes=SMALL_LIMIT),
        cost_estimate=pl.CostEstimate(
            flops=200_000, bytes_accessed=300_000, transcendentals=65536
        ),
        name="local_stats",
    )(logits)


def merge(a, b):
    top = jnp.maximum(a[0], b[0])
    return top, a[1] * jnp.exp(a[0] - top) + b[1] * jnp.exp(b[0] - top)


def merge_kernel(a_ref, b_ref, out_ref):
    out_ref[0], out_ref[1] = merge(a_ref, b_ref)


def merge_stats(a, b):
    return pl.pallas_call(
        merge_kernel,
        out_shape=jax.ShapeDtypeStruct((2, 32, 128), F32),
        compiler_params=pltpu.CompilerParams(vmem_limit_bytes=SMALL_LIMIT),
        cost_estimate=pl.CostEstimate(
            flops=20_000, bytes_accessed=100_000, transcendentals=8192
        ),
        name="merge_stats",
    )(a, b)


def weights_kernel(l_ref, a_ref, b_ref, out_ref, own_ref):
    top, total = merge(a_ref, b_ref)
    low = iota((32, 128), 1) < 64
    for k in range(8):
        a = jnp.exp(l_ref[2 * k] - top) / total
        b = jnp.exp(l_ref[2 * k + 1] - top) / total
        even = jnp.where(low, a, pltpu.roll(b, 64, 1))
        odd = jnp.where(low, pltpu.roll(a, 64, 1), b)
        block = jnp.concatenate([even[:16], odd[:16], even[16:], odd[16:]], axis=0)
        block = block.astype(BF16)
        out_ref[:, k * 128 : (k + 1) * 128] = block
        own_ref[:, k * 128 : (k + 1) * 128] = block


def softmax_weights(logits, a, b):
    return pl.pallas_call(
        weights_kernel,
        out_shape=(jax.ShapeDtypeStruct((64, 1024), BF16),) * 2,
        compiler_params=pltpu.CompilerParams(vmem_limit_bytes=SMALL_LIMIT),
        cost_estimate=pl.CostEstimate(
            flops=200_000, bytes_accessed=500_000, transcendentals=65536
        ),
        name="softmax_weights",
    )(logits, a, b)


def average_kernel(place_ref, w0, w1, w2, w3, v_ref, out_ref, wall, scr):
    side = pl.multiple_of(place_ref[4] * 32, 32)
    for k, w in enumerate((w0, w1, w2, w3)):
        start = pl.multiple_of(place_ref[k] * 32, 32)
        wall[pl.ds(start, 32), :] = w[pl.ds(side, 32), :]
    weights = wall[...]
    for c2 in range(4):
        right = jnp.concatenate(
            [v_ref[:, 2 * c2 + e].reshape(1024, 128) for e in range(2)], axis=1
        )
        part = dot(weights, right)
        for e in range(2):
            for q in range(4):
                for par in range(2):
                    row = q * 32 + par * 16
                    scr[pl.ds(q * 256 + par * 8 + 2 * c2 + e, 16, stride=16), :] = part[
                        row : row + 16, e * 128 : (e + 1) * 128
                    ]
    out_ref[...] = scr[...].astype(out_ref.dtype).reshape(32, 32, 128)


def partial_average(place, weights, values, dtype):
    vmem = pl.BlockSpec(memory_space=pltpu.VMEM)
    return pl.pallas_call(
        average_kernel,
        out_shape=jax.ShapeDtypeStruct((32, 32, 128), dtype),
        in_specs=[pl.BlockSpec(memory_space=pltpu.SMEM)] + [vmem] * 5,
        out_specs=vmem,
        scratch_shapes=[pltpu.VMEM((128, 1024), BF16), pltpu.VMEM((1024, 128), F32)],
        compiler_params=pltpu.CompilerParams(vmem_limit_bytes=SMALL_LIMIT),
        cost_estimate=pl.CostEstimate(
            flops=300_000_000, bytes_accessed=2_800_000, transcendentals=0
        ),
        name="partial_average",
    )(place, *weights, values)


def add_kernel(a_ref, b_ref, out_ref):
    out_ref[...] = (a_ref[...] + b_ref[...].astype(F32)).astype(BF16)


def add_cores(a, b):
    return pl.pallas_call(
        add_kernel,
        out_shape=jax.ShapeDtypeStruct((32, 32, 128), BF16),
        compiler_params=pltpu.CompilerParams(vmem_limit_bytes=SMALL_LIMIT),
        cost_estimate=pl.CostEstimate(
            flops=200_000, bytes_accessed=1_000_000, transcendentals=0
        ),
        name="add_cores",
    )(a, b)


def closing_kernel(p_ref, gate_ref, block_ref, out_ref, gated):
    for y in range(4):
        for x in range(4):
            head, half = 2 * y + x // 2, x % 2
            total = p_ref[y * 8 + x].astype(F32) + p_ref[y * 8 + 4 + x].astype(F32)
            cols = slice(half * 128, half * 128 + 128)
            for i in range(4):
                rows = slice(i * 64 + head * 8, i * 64 + head * 8 + 8)
                gated[rows, cols] = total[i * 8 : i * 8 + 8] * gate_ref[rows, cols]
    out_ref[...] = dot(gated[...].astype(BF16), block_ref[...], TN).astype(BF16)


def close(parts, gate, block):
    return pl.pallas_call(
        closing_kernel,
        out_shape=jax.ShapeDtypeStruct((256, 256), BF16),
        scratch_shapes=[pltpu.VMEM((256, 256), F32)],
        compiler_params=pltpu.CompilerParams(vmem_limit_bytes=SMALL_LIMIT),
        cost_estimate=pl.CostEstimate(
            flops=60_000_000, bytes_accessed=1_000_000, transcendentals=0
        ),
        name="closing",
    )(parts, gate, block)


def exchange(x, axes):
    return lax.all_to_all(x, axes, split_axis=0, concat_axis=0, tiled=True)


def shards(
    sequence_features,
    pair_window_rows,
    residue_mask,
    sequence_validity,
    pair_head_weight,
    content_projection,
    sigmoid_projection,
    closing_projection,
):
    logits = pair_logits(pair_window_rows, residue_mask.reshape(1, 64), pair_head_weight.T)
    logits = exchange(logits.reshape(16, 32, 128), GROUP)
    values = msa_values(sequence_features, content_projection)
    values = exchange(values.reshape(16, 512, 128), GROUP)
    swap = ((0, 1), (1, 0))
    mine = local_stats(logits)
    mine = merge_stats(mine, lax.ppermute(mine, "core", swap))
    weights, own = softmax_weights(logits, mine, lax.ppermute(mine, "zh", swap))
    gathered = [own] + [
        lax.ppermute(weights, "seq", [(k, (k + d) % 4) for k in range(4)])
        for d in (1, 2, 3)
    ]
    late, _ = lax.optimization_barrier((sequence_features, weights))
    gate, block = msa_gate(
        late, sequence_validity.reshape(1, 256), sigmoid_projection, closing_projection
    )
    gathered, gate, block = lax.optimization_barrier((gathered, gate, block))
    q, core = lax.axis_index("seq"), lax.axis_index("core")
    order = [(q - d) % 4 for d in range(4)]
    values = values.reshape(16, 8, 64, 128)
    theirs = partial_average(jnp.stack(order + [1 - core]), gathered, values, BF16)
    theirs = lax.ppermute(theirs, "core", swap)
    ours = partial_average(jnp.stack(order + [core]), gathered, values, F32)
    parts = exchange(add_cores(ours, theirs), CHIPS)
    return close(parts, gate, block)


def solution(mesh):
    fine = Mesh(mesh.devices.reshape(4, 4, 2, 4, 2), ("seq",) + RES)
    return jax.shard_map(
        shards,
        mesh=fine,
        in_specs=(
            P("seq", RES),
            P("seq", RES, None),
            P(RES),
            P("seq"),
            P(),
            P(),
            P(),
            P(),
        ),
        out_specs=P("seq", RES),
        check_vma=False,
    )
```

```python
import functools

import jax
import jax.numpy as jnp
from jax import lax
from jax.experimental import pallas as pl
from jax.experimental.pallas import tpu as pltpu
from jax.sharding import Mesh
from jax.sharding import PartitionSpec as P

F32 = jnp.float32
BF16 = jnp.bfloat16
EPS = 1e-05
NT = (((1,), (1,)), ((), ()))
NN = (((1,), (0,)), ((), ()))
TN = (((0,), (0,)), ((), ()))
GROUP = ("x", "y")
CHIPS = ("zh", "y", "x")
RES = ("y", "zh", "x", "core")
SMALL_LIMIT = 24 * 1024 * 1024


def dot(a, b, dims=NN):
    return lax.dot_general(a, b, dims, preferred_element_type=F32)


def iota(shape, dim):
    return lax.broadcasted_iota(jnp.int32, shape, dim)


def one_hot(cond):
    return jnp.where(cond, 1.0, 0.0).astype(BF16)


def logits_kernel(pair_ref, mask_ref, weight_ref, out_ref, scr):
    x = pair_ref[...].reshape(4096, 128)
    centered = x.astype(F32) - dot(x, jnp.full((128, 128), 1.0 / 128, BF16))
    variance = jnp.mean(centered * centered, axis=-1, keepdims=True)
    normed = (centered * lax.rsqrt(variance + EPS)).astype(BF16)
    logits = dot(weight_ref[...], normed, NT)
    mask = jnp.concatenate([mask_ref[...], mask_ref[...]], axis=1)
    for k in range(32):
        part = jnp.where(mask == 1, logits[:, k * 128 : (k + 1) * 128], -1000000000.0)
        row = (k // 2 % 2) * 16 + k // 4 * 2 + k % 2
        scr[pl.ds(row, 8, stride=32), :] = part
    block = scr[...].reshape(8, 32, 128)
    for sg in range(2):
        out_ref[:, sg] = block


def pair_logits(pair, mask, weight_t):
    return pl.pallas_call(
        logits_kernel,
        grid=(1,),
        out_shape=jax.ShapeDtypeStruct((8, 2, 32, 128), F32),
        in_specs=[
            pl.BlockSpec((64, 64, 128), lambda i: (0, 0, 0)),
            pl.BlockSpec((1, 64), lambda i: (0, 0)),
            pl.BlockSpec((8, 128), lambda i: (0, 0)),
        ],
        out_specs=pl.BlockSpec((8, 2, 32, 128), lambda i: (0, 0, 0, 0)),
        scratch_shapes=[pltpu.VMEM((256, 128), F32)],
        cost_estimate=pl.CostEstimate(
            flops=400_000_000, bytes_accessed=1_400_000, transcendentals=500_000
        ),
        name="pair_logits",
    )(pair, mask, weight_t)


def diagonal(matrix, transposed=False, by_column=False):
    rows = iota((256, 64), 0)
    spread = one_hot((rows // 4 if by_column else rows % 64) == iota((256, 64), 1))
    rep = dot(spread, matrix, NT if transposed else NN).astype(BF16)
    tile = one_hot(iota((64, 256), 1) % 64 == iota((64, 256), 0))
    copy = iota((256, 256), 0)
    copy = copy % 4 if by_column else copy // 64
    return jnp.where(copy == iota((256, 256), 1) // 64, dot(rep, tile), 0.0).astype(BF16)


def normed_columns(block):
    xt = block.T.astype(F32).reshape(4, 64, 256)
    mean = jnp.sum(xt, axis=1, keepdims=True) * (1.0 / 64)
    centered = xt - mean
    variance = jnp.sum(centered * centered, axis=1, keepdims=True) * (1.0 / 64)
    return (centered * lax.rsqrt(variance + EPS)).astype(BF16).reshape(256, 256)


def values_kernel(m_ref, content_ref, v_ref, block):
    @pl.when(pl.program_id(0) == 0)
    def _():
        block[...] = diagonal(content_ref[...], transposed=True, by_column=True)

    low = iota((32, 8, 256), 1) < 4
    for part in range(m_ref.shape[1] // 1024):
        eights = []
        for k in range(2):
            start = part * 1024 + k * 512
            a, b = (
                dot(block[...], normed_columns(m_ref[:, at : at + 256])).reshape(32, 8, 256)
                for at in (start, start + 256)
            )
            even = jnp.where(low, a, pltpu.roll(b, 4, 1))
            odd = jnp.where(low, pltpu.roll(a, 4, 1), b)
            eights.append(jnp.stack([even, odd], axis=1).reshape(64, 8, 256))
        both = jnp.concatenate(eights, axis=1).astype(BF16).reshape(8, 8, 16, 256)
        rows = slice(part * 16, part * 16 + 16)
        v_ref[:, 0, :, rows] = both[..., :128]
        v_ref[:, 1, :, rows] = both[..., 128:]


def msa_values(m, content):
    return pl.pallas_call(
        values_kernel,
        grid=(2,),
        out_shape=jax.ShapeDtypeStruct((8, 2, 8, 64, 128), BF16),
        in_specs=[
            pl.BlockSpec((256, 2048), lambda i: (0, i)),
            pl.BlockSpec((64, 64), lambda i: (0, 0)),
        ],
        out_specs=pl.BlockSpec((8, 2, 8, 32, 128), lambda i: (0, 0, 0, i, 0)),
        scratch_shapes=[pltpu.VMEM((256, 256), BF16)],
        cost_estimate=pl.CostEstimate(
            flops=2_000_000_000, bytes_accessed=4_500_000, transcendentals=100_000
        ),
        name="msa_values",
    )(m, content)


def gate_kernel(m_ref, valid_ref, sigmoid_ref, closing_ref, gate_ref, block_ref):
    inner = dot(diagonal(sigmoid_ref[...], transposed=True), normed_columns(m_ref[...]))
    gate_ref[...] = jax.nn.sigmoid(inner) * valid_ref[...].astype(F32)
    block_ref[...] = diagonal(closing_ref[...])


def msa_gate(m, valid, sigmoid, closing):
    whole = lambda i: (0, 0)
    return pl.pallas_call(
        gate_kernel,
        grid=(1,),
        out_shape=(
            jax.ShapeDtypeStruct((256, 256), F32),
            jax.ShapeDtypeStruct((256, 256), BF16),
        ),
        in_specs=[
            pl.BlockSpec((256, 256), whole),
            pl.BlockSpec((1, 256), whole),
            pl.BlockSpec((64, 64), whole),
            pl.BlockSpec((64, 64), whole),
        ],
        out_specs=(pl.BlockSpec((256, 256), whole), pl.BlockSpec((256, 256), whole)),
        cost_estimate=pl.CostEstimate(
            flops=100_000_000, bytes_accessed=600_000, transcendentals=100_000
        ),
        name="msa_gate",
    )(m, valid, sigmoid, closing)


def by_halves(x, reduce):
    low = iota(x.shape, 1) < 64
    a = reduce(x[:, :64], axis=1, keepdims=True)
    b = reduce(x[:, 64:], axis=1, keepdims=True)
    return jnp.where(low, a, b)


def stats_kernel(l_ref, out_ref):
    logits = l_ref[...]
    top = by_halves(jnp.max(logits, axis=0), jnp.max)
    total = by_halves(jnp.sum(jnp.exp(logits - top[None]), axis=0), jnp.sum)
    out_ref[0] = top
    out_ref[1] = total


def local_stats(logits):
    return pl.pallas_call(
        stats_kernel,
        out_shape=jax.ShapeDtypeStruct((2, 32, 128), F32),
        compiler_params=pltpu.CompilerParams(vmem_limit_bytes=SMALL_LIMIT),
        cost_estimate=pl.CostEstimate(
            flops=200_000, bytes_accessed=300_000, transcendentals=65536
        ),
        name="local_stats",
    )(logits)


def merge(a, b):
    top = jnp.maximum(a[0], b[0])
    return top, a[1] * jnp.exp(a[0] - top) + b[1] * jnp.exp(b[0] - top)


def merge_kernel(a_ref, b_ref, out_ref):
    out_ref[0], out_ref[1] = merge(a_ref, b_ref)


def merge_stats(a, b):
    return pl.pallas_call(
        merge_kernel,
        out_shape=jax.ShapeDtypeStruct((2, 32, 128), F32),
        compiler_params=pltpu.CompilerParams(vmem_limit_bytes=SMALL_LIMIT),
        cost_estimate=pl.CostEstimate(
            flops=20_000, bytes_accessed=100_000, transcendentals=8192
        ),
        name="merge_stats",
    )(a, b)


def weights_kernel(l_ref, a_ref, b_ref, out_ref, own_ref):
    top, total = merge(a_ref, b_ref)
    low = iota((32, 128), 1) < 64
    for k in range(8):
        a = jnp.exp(l_ref[2 * k] - top) / total
        b = jnp.exp(l_ref[2 * k + 1] - top) / total
        even = jnp.where(low, a, pltpu.roll(b, 64, 1))
        odd = jnp.where(low, pltpu.roll(a, 64, 1), b)
        block = jnp.concatenate([even[:16], odd[:16], even[16:], odd[16:]], axis=0)
        block = block.astype(BF16)
        out_ref[:, k * 128 : (k + 1) * 128] = block
        own_ref[:, k * 128 : (k + 1) * 128] = block


def softmax_weights(logits, a, b):
    return pl.pallas_call(
        weights_kernel,
        out_shape=(jax.ShapeDtypeStruct((64, 1024), BF16),) * 2,
        compiler_params=pltpu.CompilerParams(vmem_limit_bytes=SMALL_LIMIT),
        cost_estimate=pl.CostEstimate(
            flops=200_000, bytes_accessed=500_000, transcendentals=65536
        ),
        name="softmax_weights",
    )(logits, a, b)


def average_kernel(place_ref, w0, w1, w2, w3, v_ref, out_ref, wall, scr):
    side = pl.multiple_of(place_ref[4] * 32, 32)
    for k, w in enumerate((w0, w1, w2, w3)):
        start = pl.multiple_of(place_ref[k] * 32, 32)
        wall[pl.ds(start, 32), :] = w[pl.ds(side, 32), :]
    weights = wall[...]
    for c2 in range(4):
        right = jnp.concatenate(
            [v_ref[:, 2 * c2 + e].reshape(1024, 128) for e in range(2)], axis=1
        )
        part = dot(weights, right)
        for e in range(2):
            for q in range(4):
                for par in range(2):
                    row = q * 32 + par * 16
                    scr[pl.ds(q * 256 + par * 8 + 2 * c2 + e, 16, stride=16), :] = part[
                        row : row + 16, e * 128 : (e + 1) * 128
                    ]
    for y in range(4):
        for zh in range(2):
            for x in range(4):
                start = (y * 8 + zh * 4 + x) * 32
                out_ref[y * 4 + zh * 16 + x * 1] = scr[start : start + 32].astype(out_ref.dtype)


def partial_average(place, weights, values, dtype):
    vmem = pl.BlockSpec(memory_space=pltpu.VMEM)
    return pl.pallas_call(
        average_kernel,
        out_shape=jax.ShapeDtypeStruct((32, 32, 128), dtype),
        in_specs=[pl.BlockSpec(memory_space=pltpu.SMEM)] + [vmem] * 5,
        out_specs=vmem,
        scratch_shapes=[pltpu.VMEM((128, 1024), BF16), pltpu.VMEM((1024, 128), F32)],
        compiler_params=pltpu.CompilerParams(vmem_limit_bytes=SMALL_LIMIT),
        cost_estimate=pl.CostEstimate(
            flops=300_000_000, bytes_accessed=2_800_000, transcendentals=0
        ),
        name="partial_average",
    )(place, *weights, values)


def add_kernel(a_ref, b_ref, out_ref):
    out_ref[...] = (a_ref[...] + b_ref[...].astype(F32)).astype(BF16)


def add_cores(a, b):
    return pl.pallas_call(
        add_kernel,
        out_shape=jax.ShapeDtypeStruct((32, 32, 128), BF16),
        compiler_params=pltpu.CompilerParams(vmem_limit_bytes=SMALL_LIMIT),
        cost_estimate=pl.CostEstimate(
            flops=200_000, bytes_accessed=1_000_000, transcendentals=0
        ),
        name="add_cores",
    )(a, b)


def closing_kernel(p_ref, gate_ref, block_ref, out_ref, gated):
    for y in range(4):
        for x in range(4):
            head, half = 2 * x + y // 2, y % 2
            total = sum(
                p_ref[y * 4 + zh * 16 + x * 1].astype(F32) for zh in range(2)
            )
            cols = slice(half * 128, half * 128 + 128)
            for i in range(4):
                rows = slice(i * 64 + head * 8, i * 64 + head * 8 + 8)
                gated[rows, cols] = total[i * 8 : i * 8 + 8] * gate_ref[rows, cols]
    out_ref[...] = dot(gated[...].astype(BF16), block_ref[...], TN).astype(BF16)


def close(parts, gate, block):
    return pl.pallas_call(
        closing_kernel,
        out_shape=jax.ShapeDtypeStruct((256, 256), BF16),
        scratch_shapes=[pltpu.VMEM((256, 256), F32)],
        compiler_params=pltpu.CompilerParams(vmem_limit_bytes=SMALL_LIMIT),
        cost_estimate=pl.CostEstimate(
            flops=60_000_000, bytes_accessed=1_000_000, transcendentals=0
        ),
        name="closing",
    )(parts, gate, block)


def exchange(x, axes):
    return lax.all_to_all(x, axes, split_axis=0, concat_axis=0, tiled=True)


def shards(
    sequence_features,
    pair_window_rows,
    residue_mask,
    sequence_validity,
    pair_head_weight,
    content_projection,
    sigmoid_projection,
    closing_projection,
):
    logits = pair_logits(pair_window_rows, residue_mask.reshape(1, 64), pair_head_weight.T)
    logits = exchange(logits.reshape(16, 32, 128), GROUP)
    values = msa_values(sequence_features, content_projection)
    values = exchange(values.reshape(16, 512, 128), GROUP)
    swap = ((0, 1), (1, 0))
    mine = local_stats(logits)
    mine = merge_stats(mine, lax.ppermute(mine, "core", swap))
    weights, own = softmax_weights(logits, mine, lax.ppermute(mine, "zh", swap))
    gathered = [own] + [
        lax.ppermute(weights, "seq", [(k, (k + d) % 4) for k in range(4)])
        for d in (1, 2, 3)
    ]
    late, _ = lax.optimization_barrier((sequence_features, weights))
    gate, block = msa_gate(
        late, sequence_validity.reshape(1, 256), sigmoid_projection, closing_projection
    )
    gathered, gate, block = lax.optimization_barrier((gathered, gate, block))
    q, core = lax.axis_index("seq"), lax.axis_index("core")
    order = [(q - d) % 4 for d in range(4)]
    values = values.reshape(16, 8, 64, 128)
    theirs = partial_average(jnp.stack(order + [1 - core]), gathered, values, BF16)
    theirs = lax.ppermute(theirs, "core", swap)
    ours = partial_average(jnp.stack(order + [core]), gathered, values, F32)
    parts = exchange(add_cores(ours, theirs), CHIPS)
    return close(parts, gate, block)


def solution(mesh):
    fine = Mesh(mesh.devices.reshape(4, 4, 2, 4, 2), ("seq",) + RES)
    return jax.shard_map(
        shards,
        mesh=fine,
        in_specs=(
            P("seq", RES),
            P("seq", RES, None),
            P(RES),
            P("seq"),
            P(),
            P(),
            P(),
            P(),
        ),
        out_specs=P("seq", RES),
        check_vma=False,
    )
```

```python
import functools

import jax
import jax.numpy as jnp
from jax import lax
from jax.experimental import pallas as pl
from jax.experimental.pallas import tpu as pltpu
from jax.sharding import Mesh
from jax.sharding import PartitionSpec as P

F32 = jnp.float32
BF16 = jnp.bfloat16
EPS = 1e-05
NT = (((1,), (1,)), ((), ()))
NN = (((1,), (0,)), ((), ()))
TN = (((0,), (0,)), ((), ()))
GROUP = ("x", "y")
RES = ("y", "zh", "x", "core")
SMALL_LIMIT = 24 * 1024 * 1024


def dot(a, b, dims=NN):
    return lax.dot_general(a, b, dims, preferred_element_type=F32)


def iota(shape, dim):
    return lax.broadcasted_iota(jnp.int32, shape, dim)


def one_hot(cond):
    return jnp.where(cond, 1.0, 0.0).astype(BF16)


def logits_kernel(pair_ref, mask_ref, weight_ref, out_ref, scr):
    x = pair_ref[...].reshape(4096, 128)
    centered = x.astype(F32) - dot(x, jnp.full((128, 128), 1.0 / 128, BF16))
    variance = jnp.mean(centered * centered, axis=-1, keepdims=True)
    normed = (centered * lax.rsqrt(variance + EPS)).astype(BF16)
    logits = dot(weight_ref[...], normed, NT)
    mask = jnp.concatenate([mask_ref[...], mask_ref[...]], axis=1)
    for k in range(32):
        part = jnp.where(mask == 1, logits[:, k * 128 : (k + 1) * 128], -1000000000.0)
        row = (k // 2 % 2) * 16 + k // 4 * 2 + k % 2
        scr[pl.ds(row, 8, stride=32), :] = part
    block = scr[...].reshape(8, 32, 128)
    for sg in range(2):
        out_ref[:, sg] = block


def pair_logits(pair, mask, weight_t):
    return pl.pallas_call(
        logits_kernel,
        grid=(1,),
        out_shape=jax.ShapeDtypeStruct((8, 2, 32, 128), F32),
        in_specs=[
            pl.BlockSpec((64, 64, 128), lambda i: (0, 0, 0)),
            pl.BlockSpec((1, 64), lambda i: (0, 0)),
            pl.BlockSpec((8, 128), lambda i: (0, 0)),
        ],
        out_specs=pl.BlockSpec((8, 2, 32, 128), lambda i: (0, 0, 0, 0)),
        scratch_shapes=[pltpu.VMEM((256, 128), F32)],
        cost_estimate=pl.CostEstimate(
            flops=400_000_000, bytes_accessed=1_400_000, transcendentals=500_000
        ),
        name="pair_logits",
    )(pair, mask, weight_t)


def diagonal(matrix, transposed=False, by_column=False):
    rows = iota((256, 64), 0)
    spread = one_hot((rows // 4 if by_column else rows % 64) == iota((256, 64), 1))
    rep = dot(spread, matrix, NT if transposed else NN).astype(BF16)
    tile = one_hot(iota((64, 256), 1) % 64 == iota((64, 256), 0))
    copy = iota((256, 256), 0)
    copy = copy % 4 if by_column else copy // 64
    return jnp.where(copy == iota((256, 256), 1) // 64, dot(rep, tile), 0.0).astype(BF16)


def normed_columns(block):
    xt = block.T.astype(F32).reshape(4, 64, 256)
    mean = jnp.sum(xt, axis=1, keepdims=True) * (1.0 / 64)
    centered = xt - mean
    variance = jnp.sum(centered * centered, axis=1, keepdims=True) * (1.0 / 64)
    return (centered * lax.rsqrt(variance + EPS)).astype(BF16).reshape(256, 256)


def values_kernel(m_ref, content_ref, v_ref, block):
    @pl.when(pl.program_id(0) == 0)
    def _():
        block[...] = diagonal(content_ref[...], transposed=True, by_column=True)

    low = iota((32, 8, 256), 1) < 4
    for part in range(m_ref.shape[1] // 1024):
        eights = []
        for k in range(2):
            start = part * 1024 + k * 512
            a, b = (
                dot(block[...], normed_columns(m_ref[:, at : at + 256])).reshape(32, 8, 256)
                for at in (start, start + 256)
            )
            even = jnp.where(low, a, pltpu.roll(b, 4, 1))
            odd = jnp.where(low, pltpu.roll(a, 4, 1), b)
            eights.append(jnp.stack([even, odd], axis=1).reshape(64, 8, 256))
        both = jnp.concatenate(eights, axis=1).astype(BF16).reshape(8, 8, 16, 256)
        rows = slice(part * 16, part * 16 + 16)
        v_ref[:, 0, :, rows] = both[..., :128]
        v_ref[:, 1, :, rows] = both[..., 128:]


def msa_values(m, content):
    return pl.pallas_call(
        values_kernel,
        grid=(2,),
        out_shape=jax.ShapeDtypeStruct((8, 2, 8, 64, 128), BF16),
        in_specs=[
            pl.BlockSpec((256, 2048), lambda i: (0, i)),
            pl.BlockSpec((64, 64), lambda i: (0, 0)),
        ],
        out_specs=pl.BlockSpec((8, 2, 8, 32, 128), lambda i: (0, 0, 0, i, 0)),
        scratch_shapes=[pltpu.VMEM((256, 256), BF16)],
        cost_estimate=pl.CostEstimate(
            flops=2_000_000_000, bytes_accessed=4_500_000, transcendentals=100_000
        ),
        name="msa_values",
    )(m, content)


def gate_kernel(m_ref, valid_ref, sigmoid_ref, closing_ref, gate_ref, block_ref):
    inner = dot(diagonal(sigmoid_ref[...], transposed=True), normed_columns(m_ref[...]))
    gate_ref[...] = jax.nn.sigmoid(inner) * valid_ref[...].astype(F32)
    block_ref[...] = diagonal(closing_ref[...])


def msa_gate(m, valid, sigmoid, closing):
    whole = lambda i: (0, 0)
    return pl.pallas_call(
        gate_kernel,
        grid=(1,),
        out_shape=(
            jax.ShapeDtypeStruct((256, 256), F32),
            jax.ShapeDtypeStruct((256, 256), BF16),
        ),
        in_specs=[
            pl.BlockSpec((256, 256), whole),
            pl.BlockSpec((1, 256), whole),
            pl.BlockSpec((64, 64), whole),
            pl.BlockSpec((64, 64), whole),
        ],
        out_specs=(pl.BlockSpec((256, 256), whole), pl.BlockSpec((256, 256), whole)),
        cost_estimate=pl.CostEstimate(
            flops=100_000_000, bytes_accessed=600_000, transcendentals=100_000
        ),
        name="msa_gate",
    )(m, valid, sigmoid, closing)


def by_halves(x, reduce):
    low = iota(x.shape, 1) < 64
    a = reduce(x[:, :64], axis=1, keepdims=True)
    b = reduce(x[:, 64:], axis=1, keepdims=True)
    return jnp.where(low, a, b)


def stats_kernel(l_ref, out_ref):
    logits = l_ref[...]
    top = by_halves(jnp.max(logits, axis=0), jnp.max)
    total = by_halves(jnp.sum(jnp.exp(logits - top[None]), axis=0), jnp.sum)
    out_ref[0] = top
    out_ref[1] = total


def local_stats(logits):
    return pl.pallas_call(
        stats_kernel,
        out_shape=jax.ShapeDtypeStruct((2, 32, 128), F32),
        compiler_params=pltpu.CompilerParams(vmem_limit_bytes=SMALL_LIMIT),
        cost_estimate=pl.CostEstimate(
            flops=200_000, bytes_accessed=300_000, transcendentals=65536
        ),
        name="local_stats",
    )(logits)


def merge(a, b):
    top = jnp.maximum(a[0], b[0])
    return top, a[1] * jnp.exp(a[0] - top) + b[1] * jnp.exp(b[0] - top)


def merge_kernel(a_ref, b_ref, out_ref):
    out_ref[0], out_ref[1] = merge(a_ref, b_ref)


def merge_stats(a, b):
    return pl.pallas_call(
        merge_kernel,
        out_shape=jax.ShapeDtypeStruct((2, 32, 128), F32),
        compiler_params=pltpu.CompilerParams(vmem_limit_bytes=SMALL_LIMIT),
        cost_estimate=pl.CostEstimate(
            flops=20_000, bytes_accessed=100_000, transcendentals=8192
        ),
        name="merge_stats",
    )(a, b)


def weights_kernel(l_ref, a_ref, b_ref, out_ref, own_ref):
    top, total = merge(a_ref, b_ref)
    low = iota((32, 128), 1) < 64
    for k in range(8):
        a = jnp.exp(l_ref[2 * k] - top) / total
        b = jnp.exp(l_ref[2 * k + 1] - top) / total
        even = jnp.where(low, a, pltpu.roll(b, 64, 1))
        odd = jnp.where(low, pltpu.roll(a, 64, 1), b)
        block = jnp.concatenate([even[:16], odd[:16], even[16:], odd[16:]], axis=0)
        block = block.astype(BF16)
        out_ref[:, k * 128 : (k + 1) * 128] = block
        own_ref[:, k * 128 : (k + 1) * 128] = block


def softmax_weights(logits, a, b):
    return pl.pallas_call(
        weights_kernel,
        out_shape=(jax.ShapeDtypeStruct((64, 1024), BF16),) * 2,
        compiler_params=pltpu.CompilerParams(vmem_limit_bytes=SMALL_LIMIT),
        cost_estimate=pl.CostEstimate(
            flops=200_000, bytes_accessed=500_000, transcendentals=65536
        ),
        name="softmax_weights",
    )(logits, a, b)


def average_kernel(place_ref, w0, w1, w2, w3, v_ref, out_ref, wall, scr):
    side = pl.multiple_of(place_ref[4] * 32, 32)
    for k, w in enumerate((w0, w1, w2, w3)):
        start = pl.multiple_of(place_ref[k] * 32, 32)
        wall[pl.ds(start, 32), :] = w[pl.ds(side, 32), :]
    weights = wall[...]
    for c2 in range(4):
        right = jnp.concatenate(
            [v_ref[:, 2 * c2 + e].reshape(1024, 128) for e in range(2)], axis=1
        )
        part = dot(weights, right)
        for e in range(2):
            for q in range(4):
                for par in range(2):
                    row = q * 32 + par * 16
                    scr[pl.ds(q * 256 + par * 8 + 2 * c2 + e, 16, stride=16), :] = part[
                        row : row + 16, e * 128 : (e + 1) * 128
                    ]
    for y in range(4):
        for zh in range(2):
            for x in range(4):
                start = (y * 8 + zh * 4 + x) * 32
                out_ref[zh * 16 + x * 4 + y] = scr[start : start + 32].astype(out_ref.dtype)


def partial_average(place, weights, values, dtype):
    vmem = pl.BlockSpec(memory_space=pltpu.VMEM)
    return pl.pallas_call(
        average_kernel,
        out_shape=jax.ShapeDtypeStruct((32, 32, 128), dtype),
        in_specs=[pl.BlockSpec(memory_space=pltpu.SMEM)] + [vmem] * 5,
        out_specs=vmem,
        scratch_shapes=[pltpu.VMEM((128, 1024), BF16), pltpu.VMEM((1024, 128), F32)],
        compiler_params=pltpu.CompilerParams(vmem_limit_bytes=SMALL_LIMIT),
        cost_estimate=pl.CostEstimate(
            flops=300_000_000, bytes_accessed=2_800_000, transcendentals=0
        ),
        name="partial_average",
    )(place, *weights, values)


def add_kernel(a_ref, b_ref, own_ref, cross_ref):
    zh = lax.axis_index("zh")
    own = pl.ds(pl.multiple_of(zh * 16, 16), 16)
    cross = pl.ds(pl.multiple_of(16 - zh * 16, 16), 16)
    own_ref[...] = a_ref[own] + b_ref[own].astype(F32)
    cross_ref[...] = (a_ref[cross] + b_ref[cross].astype(F32)).astype(BF16)


def add_cores(a, b):
    return pl.pallas_call(
        add_kernel,
        out_shape=(
            jax.ShapeDtypeStruct((16, 32, 128), F32),
            jax.ShapeDtypeStruct((16, 32, 128), BF16),
        ),
        compiler_params=pltpu.CompilerParams(vmem_limit_bytes=SMALL_LIMIT),
        cost_estimate=pl.CostEstimate(
            flops=200_000, bytes_accessed=1_000_000, transcendentals=0
        ),
        name="add_cores",
    )(a, b)


def join_kernel(a_ref, b_ref, out_ref):
    out_ref[...] = (a_ref[...] + b_ref[...].astype(F32)).astype(BF16)


def add_halves(a, b):
    return pl.pallas_call(
        join_kernel,
        out_shape=jax.ShapeDtypeStruct((16, 32, 128), BF16),
        compiler_params=pltpu.CompilerParams(vmem_limit_bytes=SMALL_LIMIT),
        cost_estimate=pl.CostEstimate(
            flops=100_000, bytes_accessed=500_000, transcendentals=0
        ),
        name="add_halves",
    )(a, b)


def closing_kernel(p_ref, gate_ref, block_ref, out_ref, gated):
    for y in range(4):
        for x in range(4):
            head, half = 2 * x + y // 2, y % 2
            total = p_ref[x * 4 + y].astype(F32)
            cols = slice(half * 128, half * 128 + 128)
            for i in range(4):
                rows = slice(i * 64 + head * 8, i * 64 + head * 8 + 8)
                gated[rows, cols] = total[i * 8 : i * 8 + 8] * gate_ref[rows, cols]
    out_ref[...] = dot(gated[...].astype(BF16), block_ref[...], TN).astype(BF16)


def close(parts, gate, block):
    return pl.pallas_call(
        closing_kernel,
        out_shape=jax.ShapeDtypeStruct((256, 256), BF16),
        scratch_shapes=[pltpu.VMEM((256, 256), F32)],
        compiler_params=pltpu.CompilerParams(vmem_limit_bytes=SMALL_LIMIT),
        cost_estimate=pl.CostEstimate(
            flops=60_000_000, bytes_accessed=1_000_000, transcendentals=0
        ),
        name="closing",
    )(parts, gate, block)


def exchange(x, axes):
    return lax.all_to_all(x, axes, split_axis=0, concat_axis=0, tiled=True)


def shards(
    sequence_features,
    pair_window_rows,
    residue_mask,
    sequence_validity,
    pair_head_weight,
    content_projection,
    sigmoid_projection,
    closing_projection,
):
    logits = pair_logits(pair_window_rows, residue_mask.reshape(1, 64), pair_head_weight.T)
    logits = exchange(logits.reshape(16, 32, 128), GROUP)
    values = msa_values(sequence_features, content_projection)
    values = exchange(values.reshape(16, 512, 128), GROUP)
    swap = ((0, 1), (1, 0))
    mine = local_stats(logits)
    mine = merge_stats(mine, lax.ppermute(mine, "core", swap))
    weights, own = softmax_weights(logits, mine, lax.ppermute(mine, "zh", swap))
    gathered = [own] + [
        lax.ppermute(weights, "seq", [(k, (k + d) % 4) for k in range(4)])
        for d in (1, 2, 3)
    ]
    late, _ = lax.optimization_barrier((sequence_features, weights))
    gate, block = msa_gate(
        late, sequence_validity.reshape(1, 256), sigmoid_projection, closing_projection
    )
    gathered, gate, block = lax.optimization_barrier((gathered, gate, block))
    q, core = lax.axis_index("seq"), lax.axis_index("core")
    order = [(q - d) % 4 for d in range(4)]
    values = values.reshape(16, 8, 64, 128)
    theirs = partial_average(jnp.stack(order + [1 - core]), gathered, values, BF16)
    theirs = lax.ppermute(theirs, "core", swap)
    ours = partial_average(jnp.stack(order + [core]), gathered, values, F32)
    mine, cross = add_cores(ours, theirs)
    parts = exchange(add_halves(mine, lax.ppermute(cross, "zh", swap)), GROUP)
    return close(parts, gate, block)


def solution(mesh):
    fine = Mesh(mesh.devices.reshape(4, 4, 2, 4, 2), ("seq",) + RES)
    return jax.shard_map(
        shards,
        mesh=fine,
        in_specs=(
            P("seq", RES),
            P("seq", RES, None),
            P(RES),
            P("seq"),
            P(),
            P(),
            P(),
            P(),
        ),
        out_specs=P("seq", RES),
        check_vma=False,
    )
```

```python
import functools

import jax
import jax.numpy as jnp
from jax import lax
from jax.experimental import pallas as pl
from jax.experimental.pallas import tpu as pltpu
from jax.sharding import Mesh
from jax.sharding import PartitionSpec as P

F32 = jnp.float32
BF16 = jnp.bfloat16
EPS = 1e-05
NT = (((1,), (1,)), ((), ()))
NN = (((1,), (0,)), ((), ()))
TN = (((0,), (0,)), ((), ()))
GROUP = ("x", "y")
RES = ("y", "zh", "x", "core")
SMALL_LIMIT = 24 * 1024 * 1024


def dot(a, b, dims=NN):
    return lax.dot_general(a, b, dims, preferred_element_type=F32)


def iota(shape, dim):
    return lax.broadcasted_iota(jnp.int32, shape, dim)


def one_hot(cond):
    return jnp.where(cond, 1.0, 0.0).astype(BF16)


def logits_kernel(low_ref, high_ref, mask_ref, weight_ref, out_ref, scr):
    halves = [ref[...].reshape(2048, 128) for ref in (low_ref, high_ref)]
    x = jnp.concatenate(halves, axis=0)
    centered = x.astype(F32) - dot(x, jnp.full((128, 128), 1.0 / 128, BF16))
    variance = jnp.mean(centered * centered, axis=-1, keepdims=True)
    normed = (centered * lax.rsqrt(variance + EPS)).astype(BF16)
    logits = dot(weight_ref[...], normed, NT)
    mask = jnp.concatenate([mask_ref[...], mask_ref[...]], axis=1)
    for k in range(32):
        part = jnp.where(mask == 1, logits[:, k * 128 : (k + 1) * 128], -1000000000.0)
        row = (k // 2 % 2) * 16 + k // 4 * 2 + k % 2
        scr[pl.ds(row, 8, stride=32), :] = part
    block = scr[...].reshape(8, 32, 128)
    for sg in range(2):
        out_ref[:, sg] = block


def pair_logits(pair, mask, weight_t):
    return pl.pallas_call(
        logits_kernel,
        grid=(1,),
        out_shape=jax.ShapeDtypeStruct((8, 2, 32, 128), F32),
        in_specs=[
            pl.BlockSpec((32, 64, 128), lambda i: (0, 0, 0)),
            pl.BlockSpec((32, 64, 128), lambda i: (1, 0, 0)),
            pl.BlockSpec((1, 64), lambda i: (0, 0)),
            pl.BlockSpec((8, 128), lambda i: (0, 0)),
        ],
        out_specs=pl.BlockSpec((8, 2, 32, 128), lambda i: (0, 0, 0, 0)),
        scratch_shapes=[pltpu.VMEM((256, 128), F32)],
        cost_estimate=pl.CostEstimate(
            flops=400_000_000, bytes_accessed=1_400_000, transcendentals=500_000
        ),
        name="pair_logits",
    )(pair, pair, mask, weight_t)


def diagonal(matrix, transposed=False, by_column=False):
    rows = iota((256, 64), 0)
    spread = one_hot((rows // 4 if by_column else rows % 64) == iota((256, 64), 1))
    rep = dot(spread, matrix, NT if transposed else NN).astype(BF16)
    tile = one_hot(iota((64, 256), 1) % 64 == iota((64, 256), 0))
    copy = iota((256, 256), 0)
    copy = copy % 4 if by_column else copy // 64
    return jnp.where(copy == iota((256, 256), 1) // 64, dot(rep, tile), 0.0).astype(BF16)


def normed_columns(block):
    xt = block.T.astype(F32).reshape(4, 64, 256)
    mean = jnp.sum(xt, axis=1, keepdims=True) * (1.0 / 64)
    centered = xt - mean
    variance = jnp.sum(centered * centered, axis=1, keepdims=True) * (1.0 / 64)
    return (centered * lax.rsqrt(variance + EPS)).astype(BF16).reshape(256, 256)


def values_kernel(m_ref, content_ref, v_ref, block):
    @pl.when(pl.program_id(0) == 0)
    def _():
        block[...] = diagonal(content_ref[...], transposed=True, by_column=True)

    low = iota((32, 8, 256), 1) < 4
    for part in range(m_ref.shape[1] // 1024):
        eights = []
        for k in range(2):
            start = part * 1024 + k * 512
            a, b = (
                dot(block[...], normed_columns(m_ref[:, at : at + 256])).reshape(32, 8, 256)
                for at in (start, start + 256)
            )
            even = jnp.where(low, a, pltpu.roll(b, 4, 1))
            odd = jnp.where(low, pltpu.roll(a, 4, 1), b)
            eights.append(jnp.stack([even, odd], axis=1).reshape(64, 8, 256))
        both = jnp.concatenate(eights, axis=1).astype(BF16).reshape(8, 8, 16, 256)
        rows = slice(part * 16, part * 16 + 16)
        v_ref[:, 0, :, rows] = both[..., :128]
        v_ref[:, 1, :, rows] = both[..., 128:]


def msa_values(m, content):
    return pl.pallas_call(
        values_kernel,
        grid=(2,),
        out_shape=jax.ShapeDtypeStruct((8, 2, 8, 64, 128), BF16),
        in_specs=[
            pl.BlockSpec((256, 2048), lambda i: (0, i)),
            pl.BlockSpec((64, 64), lambda i: (0, 0)),
        ],
        out_specs=pl.BlockSpec((8, 2, 8, 32, 128), lambda i: (0, 0, 0, i, 0)),
        scratch_shapes=[pltpu.VMEM((256, 256), BF16)],
        cost_estimate=pl.CostEstimate(
            flops=2_000_000_000, bytes_accessed=4_500_000, transcendentals=100_000
        ),
        name="msa_values",
    )(m, content)


def gate_kernel(m_ref, valid_ref, sigmoid_ref, closing_ref, gate_ref, block_ref):
    inner = dot(diagonal(sigmoid_ref[...], transposed=True), normed_columns(m_ref[...]))
    gate_ref[...] = jax.nn.sigmoid(inner) * valid_ref[...].astype(F32)
    block_ref[...] = diagonal(closing_ref[...])


def msa_gate(m, valid, sigmoid, closing):
    whole = lambda i: (0, 0)
    return pl.pallas_call(
        gate_kernel,
        grid=(1,),
        out_shape=(
            jax.ShapeDtypeStruct((256, 256), F32),
            jax.ShapeDtypeStruct((256, 256), BF16),
        ),
        in_specs=[
            pl.BlockSpec((256, 256), whole),
            pl.BlockSpec((1, 256), whole),
            pl.BlockSpec((64, 64), whole),
            pl.BlockSpec((64, 64), whole),
        ],
        out_specs=(pl.BlockSpec((256, 256), whole), pl.BlockSpec((256, 256), whole)),
        cost_estimate=pl.CostEstimate(
            flops=100_000_000, bytes_accessed=600_000, transcendentals=100_000
        ),
        name="msa_gate",
    )(m, valid, sigmoid, closing)


def by_halves(x, reduce):
    low = iota(x.shape, 1) < 64
    a = reduce(x[:, :64], axis=1, keepdims=True)
    b = reduce(x[:, 64:], axis=1, keepdims=True)
    return jnp.where(low, a, b)


def stats_kernel(l_ref, out_ref):
    logits = l_ref[...]
    top = by_halves(jnp.max(logits, axis=0), jnp.max)
    total = by_halves(jnp.sum(jnp.exp(logits - top[None]), axis=0), jnp.sum)
    out_ref[0] = top
    out_ref[1] = total


def local_stats(logits):
    return pl.pallas_call(
        stats_kernel,
        out_shape=jax.ShapeDtypeStruct((2, 32, 128), F32),
        compiler_params=pltpu.CompilerParams(vmem_limit_bytes=SMALL_LIMIT),
        cost_estimate=pl.CostEstimate(
            flops=200_000, bytes_accessed=300_000, transcendentals=65536
        ),
        name="local_stats",
    )(logits)


def merge(a, b):
    top = jnp.maximum(a[0], b[0])
    return top, a[1] * jnp.exp(a[0] - top) + b[1] * jnp.exp(b[0] - top)


def merge_kernel(a_ref, b_ref, out_ref):
    out_ref[0], out_ref[1] = merge(a_ref, b_ref)


def merge_stats(a, b):
    return pl.pallas_call(
        merge_kernel,
        out_shape=jax.ShapeDtypeStruct((2, 32, 128), F32),
        compiler_params=pltpu.CompilerParams(vmem_limit_bytes=SMALL_LIMIT),
        cost_estimate=pl.CostEstimate(
            flops=20_000, bytes_accessed=100_000, transcendentals=8192
        ),
        name="merge_stats",
    )(a, b)


def weights_kernel(l_ref, a_ref, b_ref, out_ref, own_ref):
    top, total = merge(a_ref, b_ref)
    low = iota((32, 128), 1) < 64
    for k in range(8):
        a = jnp.exp(l_ref[2 * k] - top) / total
        b = jnp.exp(l_ref[2 * k + 1] - top) / total
        even = jnp.where(low, a, pltpu.roll(b, 64, 1))
        odd = jnp.where(low, pltpu.roll(a, 64, 1), b)
        block = jnp.concatenate([even[:16], odd[:16], even[16:], odd[16:]], axis=0)
        block = block.astype(BF16)
        out_ref[:, k * 128 : (k + 1) * 128] = block
        own_ref[:, k * 128 : (k + 1) * 128] = block


def softmax_weights(logits, a, b):
    return pl.pallas_call(
        weights_kernel,
        out_shape=(jax.ShapeDtypeStruct((64, 1024), BF16),) * 2,
        compiler_params=pltpu.CompilerParams(vmem_limit_bytes=SMALL_LIMIT),
        cost_estimate=pl.CostEstimate(
            flops=200_000, bytes_accessed=500_000, transcendentals=65536
        ),
        name="softmax_weights",
    )(logits, a, b)


def average_kernel(other, place_ref, w0, w1, w2, w3, v_ref, out_ref, wall, scr):
    core = 1 - place_ref[4] if other else place_ref[4]
    side = pl.multiple_of(core * 32, 32)
    for k, w in enumerate((w0, w1, w2, w3)):
        start = pl.multiple_of(place_ref[k] * 32, 32)
        wall[pl.ds(start, 32), :] = w[pl.ds(side, 32), :]
    weights = wall[...]
    for c2 in range(4):
        right = jnp.concatenate(
            [v_ref[:, 2 * c2 + e].reshape(1024, 128) for e in range(2)], axis=1
        )
        part = dot(weights, right)
        for e in range(2):
            for q in range(4):
                for par in range(2):
                    row = q * 32 + par * 16
                    scr[pl.ds(q * 256 + par * 8 + 2 * c2 + e, 16, stride=16), :] = part[
                        row : row + 16, e * 128 : (e + 1) * 128
                    ]
    for y in range(4):
        for zh in range(2):
            for x in range(4):
                start = (y * 8 + zh * 4 + x) * 32
                out_ref[zh * 16 + x * 4 + y] = scr[start : start + 32].astype(out_ref.dtype)


def partial_average(place, weights, values, other):
    vmem = pl.BlockSpec(memory_space=pltpu.VMEM)
    return pl.pallas_call(
        functools.partial(average_kernel, other),
        out_shape=jax.ShapeDtypeStruct((32, 32, 128), BF16 if other else F32),
        in_specs=[pl.BlockSpec(memory_space=pltpu.SMEM)] + [vmem] * 5,
        out_specs=vmem,
        scratch_shapes=[pltpu.VMEM((128, 1024), BF16), pltpu.VMEM((1024, 128), F32)],
        compiler_params=pltpu.CompilerParams(vmem_limit_bytes=SMALL_LIMIT),
        cost_estimate=pl.CostEstimate(
            flops=300_000_000, bytes_accessed=2_800_000, transcendentals=0
        ),
        name="partial_average",
    )(place, *weights, values)


def add_kernel(a_ref, b_ref, own_ref, cross_ref):
    zh = lax.axis_index("zh")
    own = pl.ds(pl.multiple_of(zh * 16, 16), 16)
    cross = pl.ds(pl.multiple_of(16 - zh * 16, 16), 16)
    own_ref[...] = a_ref[own] + b_ref[own].astype(F32)
    cross_ref[...] = (a_ref[cross] + b_ref[cross].astype(F32)).astype(BF16)


def add_cores(a, b):
    return pl.pallas_call(
        add_kernel,
        out_shape=(
            jax.ShapeDtypeStruct((16, 32, 128), F32),
            jax.ShapeDtypeStruct((16, 32, 128), BF16),
        ),
        compiler_params=pltpu.CompilerParams(vmem_limit_bytes=SMALL_LIMIT),
        cost_estimate=pl.CostEstimate(
            flops=200_000, bytes_accessed=1_000_000, transcendentals=0
        ),
        name="add_cores",
    )(a, b)


def join_kernel(a_ref, b_ref, out_ref):
    out_ref[...] = (a_ref[...] + b_ref[...].astype(F32)).astype(BF16)


def add_halves(a, b):
    return pl.pallas_call(
        join_kernel,
        out_shape=jax.ShapeDtypeStruct((16, 32, 128), BF16),
        compiler_params=pltpu.CompilerParams(vmem_limit_bytes=SMALL_LIMIT),
        cost_estimate=pl.CostEstimate(
            flops=100_000, bytes_accessed=500_000, transcendentals=0
        ),
        name="add_halves",
    )(a, b)


def closing_kernel(p_ref, gate_ref, block_ref, out_ref, gated):
    for y in range(4):
        for x in range(4):
            head, half = 2 * x + y // 2, y % 2
            total = p_ref[x * 4 + y].astype(F32)
            cols = slice(half * 128, half * 128 + 128)
            for i in range(4):
                rows = slice(i * 64 + head * 8, i * 64 + head * 8 + 8)
                gated[rows, cols] = total[i * 8 : i * 8 + 8] * gate_ref[rows, cols]
    out_ref[...] = dot(gated[...].astype(BF16), block_ref[...], TN).astype(BF16)


def close(parts, gate, block):
    return pl.pallas_call(
        closing_kernel,
        out_shape=jax.ShapeDtypeStruct((256, 256), BF16),
        scratch_shapes=[pltpu.VMEM((256, 256), F32)],
        compiler_params=pltpu.CompilerParams(vmem_limit_bytes=SMALL_LIMIT),
        cost_estimate=pl.CostEstimate(
            flops=60_000_000, bytes_accessed=1_000_000, transcendentals=0
        ),
        name="closing",
    )(parts, gate, block)


def exchange(x, axes):
    return lax.all_to_all(x, axes, split_axis=0, concat_axis=0, tiled=True)


def shards(
    sequence_features,
    pair_window_rows,
    residue_mask,
    sequence_validity,
    pair_head_weight,
    content_projection,
    sigmoid_projection,
    closing_projection,
):
    logits = pair_logits(pair_window_rows, residue_mask.reshape(1, 64), pair_head_weight.T)
    logits = exchange(logits.reshape(16, 32, 128), GROUP)
    values = msa_values(sequence_features, content_projection)
    values = exchange(values.reshape(16, 512, 128), GROUP)
    swap = ((0, 1), (1, 0))
    mine = local_stats(logits)
    mine = merge_stats(mine, lax.ppermute(mine, "core", swap))
    weights, own = softmax_weights(logits, mine, lax.ppermute(mine, "zh", swap))
    gathered = [own] + [
        lax.ppermute(weights, "seq", [(k, (k + d) % 4) for k in range(4)])
        for d in (1, 2, 3)
    ]
    late, _ = lax.optimization_barrier((sequence_features, weights))
    gate, block = msa_gate(
        late, sequence_validity.reshape(1, 256), sigmoid_projection, closing_projection
    )
    gathered, gate, block = lax.optimization_barrier((gathered, gate, block))
    q, core = lax.axis_index("seq"), lax.axis_index("core")
    order = [(q - d) % 4 for d in range(4)]
    values = values.reshape(16, 8, 64, 128)
    place = jnp.stack(order + [core])
    theirs = partial_average(place, gathered, values, True)
    theirs = lax.ppermute(theirs, "core", swap)
    ours = partial_average(place, gathered, values, False)
    mine, cross = add_cores(ours, theirs)
    parts = exchange(add_halves(mine, lax.ppermute(cross, "zh", swap)), GROUP)
    return close(parts, gate, block)


def solution(mesh):
    fine = Mesh(mesh.devices.reshape(4, 4, 2, 4, 2), ("seq",) + RES)
    return jax.shard_map(
        shards,
        mesh=fine,
        in_specs=(
            P("seq", RES),
            P("seq", RES, None),
            P(RES),
            P("seq"),
            P(),
            P(),
            P(),
            P(),
        ),
        out_specs=P("seq", RES),
        check_vma=False,
    )
```

```python
import functools

import jax
import jax.numpy as jnp
from jax import lax
from jax.experimental import pallas as pl
from jax.experimental.pallas import tpu as pltpu
from jax.sharding import Mesh
from jax.sharding import PartitionSpec as P

F32 = jnp.float32
BF16 = jnp.bfloat16
EPS = 1e-05
NT = (((1,), (1,)), ((), ()))
NN = (((1,), (0,)), ((), ()))
TN = (((0,), (0,)), ((), ()))
GROUP = ("x", "y")
RES = ("y", "zh", "x", "core")
SMALL_LIMIT = 24 * 1024 * 1024


def dot(a, b, dims=NN):
    return lax.dot_general(a, b, dims, preferred_element_type=F32)


def iota(shape, dim):
    return lax.broadcasted_iota(jnp.int32, shape, dim)


def one_hot(cond):
    return jnp.where(cond, 1.0, 0.0).astype(BF16)


def logits_kernel(pair_ref, mask_ref, weight_ref, out_ref, scr):
    x = pair_ref[...].reshape(4096, 128)
    centered = x.astype(F32) - dot(x, jnp.full((128, 128), 1.0 / 128, BF16))
    variance = jnp.mean(centered * centered, axis=-1, keepdims=True)
    normed = (centered * lax.rsqrt(variance + EPS)).astype(BF16)
    logits = dot(weight_ref[...], normed, NT)
    mask = jnp.concatenate([mask_ref[...], mask_ref[...]], axis=1)
    for k in range(32):
        part = jnp.where(mask == 1, logits[:, k * 128 : (k + 1) * 128], -1000000000.0)
        row = (k // 2 % 2) * 16 + k // 4 * 2 + k % 2
        scr[pl.ds(row, 8, stride=32), :] = part
    block = scr[...].reshape(8, 32, 128)
    for sg in range(2):
        out_ref[:, sg] = block


def pair_logits(pair, mask, weight_t):
    return pl.pallas_call(
        logits_kernel,
        grid=(1,),
        out_shape=jax.ShapeDtypeStruct((8, 2, 32, 128), F32),
        in_specs=[
            pl.BlockSpec((64, 64, 128), lambda i: (0, 0, 0)),
            pl.BlockSpec((1, 64), lambda i: (0, 0)),
            pl.BlockSpec((8, 128), lambda i: (0, 0)),
        ],
        out_specs=pl.BlockSpec((8, 2, 32, 128), lambda i: (0, 0, 0, 0)),
        scratch_shapes=[pltpu.VMEM((256, 128), F32)],
        cost_estimate=pl.CostEstimate(
            flops=400_000_000, bytes_accessed=1_400_000, transcendentals=500_000
        ),
        name="pair_logits",
    )(pair, mask, weight_t)


def diagonal(matrix, transposed=False, by_column=False):
    rows = iota((256, 64), 0)
    spread = one_hot((rows // 4 if by_column else rows % 64) == iota((256, 64), 1))
    rep = dot(spread, matrix, NT if transposed else NN).astype(BF16)
    tile = one_hot(iota((64, 256), 1) % 64 == iota((64, 256), 0))
    copy = iota((256, 256), 0)
    copy = copy % 4 if by_column else copy // 64
    return jnp.where(copy == iota((256, 256), 1) // 64, dot(rep, tile), 0.0).astype(BF16)


def normed_columns(block):
    xt = block.T.astype(F32).reshape(4, 64, 256)
    mean = jnp.sum(xt, axis=1, keepdims=True) * (1.0 / 64)
    centered = xt - mean
    variance = jnp.sum(centered * centered, axis=1, keepdims=True) * (1.0 / 64)
    return (centered * lax.rsqrt(variance + EPS)).astype(BF16).reshape(256, 256)


def values_kernel(m_ref, content_ref, v_ref, block):
    @pl.when(pl.program_id(0) == 0)
    def _():
        block[...] = diagonal(content_ref[...], transposed=True, by_column=True)

    low = iota((32, 8, 256), 1) < 4
    for part in range(m_ref.shape[1] // 1024):
        eights = []
        for k in range(2):
            start = part * 1024 + k * 512
            a, b = (
                dot(block[...], normed_columns(m_ref[:, at : at + 256])).reshape(32, 8, 256)
                for at in (start, start + 256)
            )
            even = jnp.where(low, a, pltpu.roll(b, 4, 1))
            odd = jnp.where(low, pltpu.roll(a, 4, 1), b)
            eights.append(jnp.stack([even, odd], axis=1).reshape(64, 8, 256))
        both = jnp.concatenate(eights, axis=1).astype(BF16).reshape(8, 8, 16, 256)
        rows = slice(part * 16, part * 16 + 16)
        v_ref[:, 0, :, rows] = both[..., :128]
        v_ref[:, 1, :, rows] = both[..., 128:]


def msa_values(m, content):
    return pl.pallas_call(
        values_kernel,
        grid=(2,),
        out_shape=jax.ShapeDtypeStruct((8, 2, 8, 64, 128), BF16),
        in_specs=[
            pl.BlockSpec((256, 2048), lambda i: (0, i)),
            pl.BlockSpec((64, 64), lambda i: (0, 0)),
        ],
        out_specs=pl.BlockSpec((8, 2, 8, 32, 128), lambda i: (0, 0, 0, i, 0)),
        scratch_shapes=[pltpu.VMEM((256, 256), BF16)],
        cost_estimate=pl.CostEstimate(
            flops=2_000_000_000, bytes_accessed=4_500_000, transcendentals=100_000
        ),
        name="msa_values",
    )(m, content)


def gate_kernel(m_ref, valid_ref, sigmoid_ref, closing_ref, gate_ref, block_ref):
    inner = dot(diagonal(sigmoid_ref[...], transposed=True), normed_columns(m_ref[...]))
    gate_ref[...] = jax.nn.sigmoid(inner) * valid_ref[...].astype(F32)
    block_ref[...] = diagonal(closing_ref[...])


def msa_gate(m, valid, sigmoid, closing):
    whole = lambda i: (0, 0)
    return pl.pallas_call(
        gate_kernel,
        grid=(1,),
        out_shape=(
            jax.ShapeDtypeStruct((256, 256), F32),
            jax.ShapeDtypeStruct((256, 256), BF16),
        ),
        in_specs=[
            pl.BlockSpec((256, 256), whole),
            pl.BlockSpec((1, 256), whole),
            pl.BlockSpec((64, 64), whole),
            pl.BlockSpec((64, 64), whole),
        ],
        out_specs=(pl.BlockSpec((256, 256), whole), pl.BlockSpec((256, 256), whole)),
        cost_estimate=pl.CostEstimate(
            flops=100_000_000, bytes_accessed=600_000, transcendentals=100_000
        ),
        name="msa_gate",
    )(m, valid, sigmoid, closing)


def by_halves(x, reduce):
    low = iota(x.shape, 1) < 64
    a = reduce(x[:, :64], axis=1, keepdims=True)
    b = reduce(x[:, 64:], axis=1, keepdims=True)
    return jnp.where(low, a, b)


def stats_kernel(l_ref, out_ref):
    logits = l_ref[...]
    top = by_halves(jnp.max(logits, axis=0), jnp.max)
    total = by_halves(jnp.sum(jnp.exp(logits - top[None]), axis=0), jnp.sum)
    out_ref[0] = top
    out_ref[1] = total


def local_stats(logits):
    return pl.pallas_call(
        stats_kernel,
        out_shape=jax.ShapeDtypeStruct((2, 32, 128), F32),
        compiler_params=pltpu.CompilerParams(vmem_limit_bytes=SMALL_LIMIT),
        cost_estimate=pl.CostEstimate(
            flops=200_000, bytes_accessed=300_000, transcendentals=65536
        ),
        name="local_stats",
    )(logits)


def merge(a, b):
    top = jnp.maximum(a[0], b[0])
    return top, a[1] * jnp.exp(a[0] - top) + b[1] * jnp.exp(b[0] - top)


def merge_kernel(a_ref, b_ref, out_ref):
    out_ref[0], out_ref[1] = merge(a_ref, b_ref)


def merge_stats(a, b):
    return pl.pallas_call(
        merge_kernel,
        out_shape=jax.ShapeDtypeStruct((2, 32, 128), F32),
        compiler_params=pltpu.CompilerParams(vmem_limit_bytes=SMALL_LIMIT),
        cost_estimate=pl.CostEstimate(
            flops=20_000, bytes_accessed=100_000, transcendentals=8192
        ),
        name="merge_stats",
    )(a, b)


def weights_kernel(l_ref, a_ref, b_ref, out_ref, own_ref):
    top, total = merge(a_ref, b_ref)
    low = iota((32, 128), 1) < 64
    for k in range(8):
        a = jnp.exp(l_ref[2 * k] - top) / total
        b = jnp.exp(l_ref[2 * k + 1] - top) / total
        even = jnp.where(low, a, pltpu.roll(b, 64, 1))
        odd = jnp.where(low, pltpu.roll(a, 64, 1), b)
        eights = [
            part[core * 16 + zh * 8 : core * 16 + zh * 8 + 8]
            for zh in range(2)
            for core in range(2)
            for part in (even, odd)
        ]
        block = jnp.concatenate(eights, axis=0)
        block = block.astype(BF16)
        out_ref[:, k * 128 : (k + 1) * 128] = block
        own_ref[:, k * 128 : (k + 1) * 128] = block


def softmax_weights(logits, a, b):
    return pl.pallas_call(
        weights_kernel,
        out_shape=(jax.ShapeDtypeStruct((64, 1024), BF16),) * 2,
        compiler_params=pltpu.CompilerParams(vmem_limit_bytes=SMALL_LIMIT),
        cost_estimate=pl.CostEstimate(
            flops=200_000, bytes_accessed=500_000, transcendentals=65536
        ),
        name="softmax_weights",
    )(logits, a, b)


def average_kernel(other, place_ref, w0, w1, w2, w3, v_ref, own_ref, send_ref, wall, scr):
    core = place_ref[4]
    half = 1 - place_ref[5] if other else place_ref[5]
    side = pl.multiple_of(half * 32, 32)
    for k, w in enumerate((w0, w1, w2, w3)):
        start = pl.multiple_of(place_ref[k] * 32, 32)
        wall[pl.ds(start, 32), :] = w[pl.ds(side, 32), :]
    weights = wall[...]
    for c2 in range(4):
        right = jnp.concatenate(
            [v_ref[:, 2 * c2 + e].reshape(1024, 128) for e in range(2)], axis=1
        )
        part = dot(weights, right)
        for e in range(2):
            for q in range(4):
                for c in range(2):
                    for par in range(2):
                        row = q * 32 + c * 16 + par * 8
                        start = c * 512 + q * 128 + par * 8 + 2 * c2 + e
                        scr[pl.ds(start, 8, stride=16), :] = part[
                            row : row + 8, e * 128 : (e + 1) * 128
                        ]
    for y in range(4):
        for x in range(4):
            at = (y * 4 + x) * 32
            own = pl.multiple_of(core * 512 + at, 32)
            send = pl.multiple_of((1 - core) * 512 + at, 32)
            own_ref[x * 4 + y] = scr[pl.ds(own, 32), :]
            send_ref[x * 4 + y] = scr[pl.ds(send, 32), :].astype(BF16)


def partial_average(place, weights, values, other):
    vmem = pl.BlockSpec(memory_space=pltpu.VMEM)
    return pl.pallas_call(
        functools.partial(average_kernel, other),
        out_shape=(
            jax.ShapeDtypeStruct((16, 32, 128), F32),
            jax.ShapeDtypeStruct((16, 32, 128), BF16),
        ),
        in_specs=[pl.BlockSpec(memory_space=pltpu.SMEM)] + [vmem] * 5,
        out_specs=(vmem, vmem),
        scratch_shapes=[pltpu.VMEM((128, 1024), BF16), pltpu.VMEM((1024, 128), F32)],
        compiler_params=pltpu.CompilerParams(vmem_limit_bytes=SMALL_LIMIT),
        cost_estimate=pl.CostEstimate(
            flops=300_000_000, bytes_accessed=2_800_000, transcendentals=0
        ),
        name="partial_average",
    )(place, *weights, values)


def add_kernel(own_ref, *refs):
    total = own_ref[...]
    for ref in refs[:-1]:
        total = total + ref[...].astype(F32)
    refs[-1][...] = total.astype(BF16)


def add_parts(*parts):
    return pl.pallas_call(
        add_kernel,
        out_shape=jax.ShapeDtypeStruct((16, 32, 128), BF16),
        compiler_params=pltpu.CompilerParams(vmem_limit_bytes=SMALL_LIMIT),
        cost_estimate=pl.CostEstimate(
            flops=100_000, bytes_accessed=500_000, transcendentals=0
        ),
        name="add_parts",
    )(*parts)


def closing_kernel(p_ref, gate_ref, block_ref, out_ref, gated):
    for y in range(4):
        for x in range(4):
            head, half = 2 * x + y // 2, y % 2
            total = p_ref[x * 4 + y].astype(F32)
            cols = slice(half * 128, half * 128 + 128)
            for i in range(4):
                rows = slice(i * 64 + head * 8, i * 64 + head * 8 + 8)
                gated[rows, cols] = total[i * 8 : i * 8 + 8] * gate_ref[rows, cols]
    out_ref[...] = dot(gated[...].astype(BF16), block_ref[...], TN).astype(BF16)


def close(parts, gate, block):
    return pl.pallas_call(
        closing_kernel,
        out_shape=jax.ShapeDtypeStruct((256, 256), BF16),
        scratch_shapes=[pltpu.VMEM((256, 256), F32)],
        compiler_params=pltpu.CompilerParams(vmem_limit_bytes=SMALL_LIMIT),
        cost_estimate=pl.CostEstimate(
            flops=60_000_000, bytes_accessed=1_000_000, transcendentals=0
        ),
        name="closing",
    )(parts, gate, block)


def exchange(x, axes):
    return lax.all_to_all(x, axes, split_axis=0, concat_axis=0, tiled=True)


def shards(
    sequence_features,
    pair_window_rows,
    residue_mask,
    sequence_validity,
    pair_head_weight,
    content_projection,
    sigmoid_projection,
    closing_projection,
):
    logits = pair_logits(pair_window_rows, residue_mask.reshape(1, 64), pair_head_weight.T)
    logits = exchange(logits.reshape(16, 32, 128), GROUP)
    values = msa_values(sequence_features, content_projection)
    values = exchange(values.reshape(16, 512, 128), GROUP)
    swap = ((0, 1), (1, 0))
    mine = local_stats(logits)
    mine = merge_stats(mine, lax.ppermute(mine, "core", swap))
    weights, own = softmax_weights(logits, mine, lax.ppermute(mine, "zh", swap))
    gathered = [own] + [
        lax.ppermute(weights, "seq", [(k, (k + d) % 4) for k in range(4)])
        for d in (1, 2, 3)
    ]
    late, _ = lax.optimization_barrier((sequence_features, weights))
    gate, block = msa_gate(
        late, sequence_validity.reshape(1, 256), sigmoid_projection, closing_projection
    )
    gathered, gate, block = lax.optimization_barrier((gathered, gate, block))
    q, core = lax.axis_index("seq"), lax.axis_index("core")
    order = [(q - d) % 4 for d in range(4)]
    values = values.reshape(16, 8, 64, 128)
    place = jnp.stack(order + [core, lax.axis_index("zh")])
    far, theirs = partial_average(place, gathered, values, True)
    far = add_parts(far, lax.ppermute(theirs, "core", swap))
    far = lax.ppermute(far, "zh", swap)
    near, theirs = partial_average(place, gathered, values, False)
    parts = add_parts(near, lax.ppermute(theirs, "core", swap), far)
    parts = exchange(parts, GROUP)
    return close(parts, gate, block)


def solution(mesh):
    fine = Mesh(mesh.devices.reshape(4, 4, 2, 4, 2), ("seq",) + RES)
    return jax.shard_map(
        shards,
        mesh=fine,
        in_specs=(
            P("seq", RES),
            P("seq", RES, None),
            P(RES),
            P("seq"),
            P(),
            P(),
            P(),
            P(),
        ),
        out_specs=P("seq", RES),
        check_vma=False,
    )
```
